256 devices in a mesh: rep: 8 (over y, core), ep: 32 (over x, z).
Axes of the slice: x: 4, y: 4, z: 8, core: 2. Of those that a mesh axis runs over, the one named last changes fastest.
Arguments:
- tokens: bfloat16 [32768, 1024], P(('rep', 'ep')), may hold values from -6 to 6
- expert_ids: int32 [32768, 8], P(('rep', 'ep')), may hold values from 0 to 63, all different within a row; in each aligned block of 128 rows (0 to 127, 128 to 255, ...) at most 24 rows name the same one
- route_weights: float32 [32768, 8], P(('rep', 'ep')), may hold values from 0.03 to 0.5
- out_grad: bfloat16 [32768, 1024], P(('rep', 'ep')), may hold values from -4 to 4
- gate_weight: bfloat16 [64, 1024, 384], P('ep'), may hold values from -0.1875 to 0.1875
- up_weight: bfloat16 [64, 1024, 384], P('ep'), may hold values from -0.1875 to 0.1875
- down_weight: bfloat16 [64, 384, 1024], P('ep'), may hold values from -0.3125 to 0.3125
Outputs:
- layer_out: bfloat16 [32768, 1024], P(('rep', 'ep'))
- token_grad: bfloat16 [32768, 1024], P(('rep', 'ep'))
- route_grad: float32 [32768, 8], P(('rep', 'ep'))
- gate_weight_grad: float32 [64, 1024, 384], P('ep', 'rep')
- up_weight_grad: float32 [64, 1024, 384], P('ep', 'rep')
- down_weight_grad: float32 [64, 384, 1024], P('ep', 'rep')
The draws below stay inside these ranges and needn't reach their ends.
Inputs may be any that keep to these rules, and one draw needn't show every extreme that they name: `expert_ids`: each row names 8 different experts. Among the rows of one device (an aligned block of 128 rows) no expert is named more than 24 times, and in every draw some expert is named exactly 24 times by the rows of some device.
All inputs are finite; a program needn't handle non-finite values.
Results may differ from the reference program's by a relative error of at most 0.014.
Values may be sent and summed in bfloat16 or wider, within the bound.
A program may use at most 128 MiB of HBM per device.

```python
import math
import jax
import jax.numpy as jnp
import numpy as np
from jax import lax

D = 1024
FF = 384
TOP = 8
TOK_DEV = 128
EXPERTS = 64
TOKENS = 32768
CAP = 24
N_REP = 8
N_EP = 32


def level_of(rng, extent, shards, low, top_value):
    def one(dim, parts):
        draws = jax.random.uniform(jax.random.fold_in(jax.random.fold_in(rng, 6), dim), (parts,), jnp.float32, low / len(shards), top_value / len(shards))
        return jnp.repeat(jnp.exp(draws), extent[dim] // parts).reshape((-1,) + (1,) * (len(extent) - dim - 1))

    level = one(*shards[0])
    for cut in shards[1:]:
        level = level * one(*cut)
    return level


def shared_out(rng, own, number, rows, count, top, most, skew):
    sequence = jax.random.permutation(rng, count)
    packed, common = portions_of(count, rows * top, most, skew, True), portions_of(count, rows * top, most, skew, False)
    places = jnp.arange(count)

    def named(tallies, offset_by):
        used = int((tallies > 0).sum())
        fixed = max(1, used // 4)
        moved = fixed + (places - fixed + offset_by * (used - fixed)) % max(1, count - fixed)
        return jnp.zeros((count,), jnp.int32).at[sequence[jnp.where(places < fixed, places, moved)]].set(jnp.asarray(tallies, jnp.int32))

    tallies = jnp.where(number % 4 == 0, named(packed, number // 4), named(common, number - number // 4 - 1))
    mixed = jax.random.permutation(jax.random.fold_in(own, 3), count)
    donor, taker = mixed[0:count // 2 * 2:2], mixed[1:count // 2 * 2:2]
    slack = jnp.minimum(tallies[donor] - 1, most - tallies[taker]) // 2
    slack = jnp.where((donor == sequence[0]) | (taker == sequence[0]) | (tallies[taker] == 0), 0, jnp.maximum(slack, 0))
    moved = jax.random.randint(jax.random.fold_in(own, 4), (count // 2,), 0, 1 << 20) % (slack + 1)
    tallies = tallies.at[donor].add(-moved).at[taker].add(moved)
    labels = jnp.searchsorted(jnp.cumsum(tallies), jnp.arange(rows * top), side="right").astype(jnp.int32)
    table = labels.reshape(top, rows).T
    table = table[jax.random.permutation(jax.random.fold_in(own, 1), rows)]
    offset_by = jax.random.randint(jax.random.fold_in(own, 2), (rows, 1), 0, top)
    return jnp.take_along_axis(table, (jnp.arange(top)[None, :] + offset_by) % top, axis=1)


def portions_of(amount, total, limit, slope, full):
    loads = [(1 << 20) // math.isqrt(grade ** slope) + 1 for grade in range(1, amount + 1)]
    largest = limit if full else min(limit, max(-(-total // amount), total * loads[0] // sum(loads)))
    least = 1 if total - largest >= amount - 1 else 0
    counts, surplus = [largest] + [least] * (amount - 1), total - largest - least * (amount - 1)
    while surplus > 0:
        free = [i for i in range(1, amount) if counts[i] < largest] or [i for i in range(1, amount) if counts[i] < limit]
        mass, remaining = sum([loads[i] for i in free]), surplus
        for i in free:
            addition = min(limit - counts[i], max(1, remaining * loads[i] // mass), surplus)
            counts[i] = counts[i] + addition
            surplus = surplus - addition
    return np.array(counts)


def bell_draw(stream_key, dims, deviation, most, pieces=(), held_as=jnp.bfloat16):
    array = jax.random.normal(stream_key, dims, jnp.float32) * deviation
    if len(pieces) > 0:
        array = level_of(stream_key, dims, pieces, -0.22, 0.18) * array
    return jnp.clip(array, min=-most, max=most).astype(held_as)


def setup_inputs(seed: int = 0) -> dict:
    key_list = jax.random.split(jax.random.key(seed), 8)
    tokens = bell_draw(key_list[0], (TOKENS, D), 1.0, 6.0, ((0, 256),))
    expert_ids_keys = jax.random.split(jax.random.fold_in(key_list[1], 1), TOKENS // TOK_DEV)
    expert_ids_turns = jax.random.permutation(jax.random.fold_in(key_list[1], 3), TOKENS // TOK_DEV)
    expert_ids = jax.vmap(lambda own, number: shared_out(jax.random.fold_in(key_list[1], 2), own, number, TOK_DEV, EXPERTS, TOP, CAP, 1))(expert_ids_keys, expert_ids_turns).reshape((TOKENS, TOP))
    route_weights = jnp.clip(jnp.exp(math.log(0.5) - 2.8134107 * jax.random.uniform(key_list[2], (TOKENS, TOP), jnp.float32) ** level_of(key_list[2], (TOKENS, TOP), ((0, 256),), -0.2, 0.2)), 0.03, 0.5)
    out_grad = bell_draw(key_list[3], (TOKENS, D), 0.5, 4.0, ((0, 256),))
    gate_weight = bell_draw(key_list[4], (EXPERTS, D, FF), D ** -0.5, 0.1875, ((0, 32),))
    up_weight = bell_draw(key_list[5], (EXPERTS, D, FF), D ** -0.5, 0.1875, ((0, 32),))
    down_weight = bell_draw(key_list[6], (EXPERTS, FF, D), FF ** -0.5, 0.3125, ((0, 32),))
    return dict(tokens=tokens, expert_ids=expert_ids, route_weights=route_weights, out_grad=out_grad, gate_weight=gate_weight, up_weight=up_weight, down_weight=down_weight)


def silu_parts(gate_pre):
    sigmoid_gate = jax.nn.sigmoid(gate_pre)
    return gate_pre * sigmoid_gate, sigmoid_gate * (1.0 + gate_pre * (1.0 - sigmoid_gate))


def replica_sum(left, right):
    left_parts = left.reshape(N_REP, N_EP * CAP, left.shape[1]).astype(jnp.float32)
    right_parts = right.reshape(N_REP, N_EP * CAP, right.shape[1]).astype(jnp.float32)
    partial_sums = jnp.einsum("rna,rnb->rab", left_parts, right_parts)
    return jnp.sum(partial_sums.astype(jnp.bfloat16).astype(jnp.float32), axis=0)


def reference(tokens, expert_ids, route_weights, out_grad, gate_weight, up_weight, down_weight):
    devices_all = N_REP * N_EP
    pair_total = TOKENS * TOP
    per_block = TOK_DEV * TOP
    block_ids = expert_ids.reshape(devices_all, per_block).astype(jnp.int32)
    columns = jnp.arange(EXPERTS, dtype=jnp.int32)
    onehot = (block_ids[:, :, None] == columns[None, None, :]).astype(jnp.int32)
    slot_rank = jnp.sum((jnp.cumsum(onehot, axis=1).astype(jnp.int32) - 1) * onehot, axis=2).astype(jnp.int32)
    block_base = (jnp.arange(devices_all, dtype=jnp.int32) * CAP)[:, None]
    position = (block_ids * (devices_all * CAP) + block_base + slot_rank).reshape(-1).astype(jnp.int32)
    table = jnp.full((EXPERTS * devices_all * CAP,), pair_total, jnp.int32)
    table = table.at[position].set(jnp.arange(pair_total, dtype=jnp.int32)).reshape(EXPERTS, devices_all * CAP)
    flat_weights = route_weights.reshape(-1)
    zero_half = jnp.zeros((), jnp.bfloat16)

    def per_expert(totals, inputs):
        slot_pairs, gate_matrix, up_matrix, down_matrix = inputs
        occupied = slot_pairs < pair_total
        pair_index = jnp.where(occupied, slot_pairs, 0).astype(jnp.int32)
        token_index = (pair_index // TOP).astype(jnp.int32)
        row_mask = occupied[:, None]
        weight_col = jnp.where(occupied, flat_weights[pair_index], 0.0)
        expert_in = jnp.where(row_mask, tokens[token_index], zero_half)
        grad_rows = out_grad[token_index]
        out_rows = jnp.where(row_mask, (weight_col[:, None] * grad_rows).astype(jnp.bfloat16), zero_half)
        gate_pre = jnp.dot(expert_in, gate_matrix, preferred_element_type=jnp.float32)
        up_pre = jnp.dot(expert_in, up_matrix, preferred_element_type=jnp.float32)
        silu_gate, silu_slope = silu_parts(gate_pre)
        hidden = (silu_gate * up_pre).astype(jnp.bfloat16)
        expert_out = jnp.dot(hidden, down_matrix, preferred_element_type=jnp.float32).astype(jnp.bfloat16)
        hidden_grad = jnp.dot(out_rows, down_matrix.T, preferred_element_type=jnp.float32)
        gate_delta = (hidden_grad * up_pre * silu_slope).astype(jnp.bfloat16)
        up_delta = (hidden_grad * silu_gate).astype(jnp.bfloat16)
        in_grads = (jnp.dot(gate_delta, gate_matrix.T, preferred_element_type=jnp.float32)
                    + jnp.dot(up_delta, up_matrix.T, preferred_element_type=jnp.float32)).astype(jnp.bfloat16)
        grad_gate = replica_sum(expert_in, gate_delta)
        grad_up = replica_sum(expert_in, up_delta)
        grad_down = replica_sum(hidden, out_rows)
        layer_total, input_total, route_total = totals
        layer_total = layer_total.at[token_index].add(weight_col[:, None] * expert_out.astype(jnp.float32))
        input_total = input_total.at[token_index].add(jnp.where(row_mask, in_grads.astype(jnp.float32), 0.0))
        route_terms = jnp.sum(grad_rows.astype(jnp.float32) * expert_out.astype(jnp.float32), axis=1)
        route_total = route_total.at[pair_index].add(jnp.where(occupied, route_terms, 0.0))
        return (layer_total, input_total, route_total), (grad_gate, grad_up, grad_down)

    start = (jnp.zeros((TOKENS, D), jnp.float32), jnp.zeros((TOKENS, D), jnp.float32),
             jnp.zeros((pair_total,), jnp.float32))
    totals, grads = lax.scan(per_expert, start, (table, gate_weight, up_weight, down_weight))
    layer_total, input_total, route_total = totals
    return (layer_total.astype(jnp.bfloat16), input_total.astype(jnp.bfloat16),
            route_total.reshape(TOKENS, TOP), grads[0], grads[1], grads[2])
```

```python
import jax
import jax.numpy as jnp
from jax import lax
from jax.experimental import pallas as pl
from jax.experimental.pallas import tpu as pltpu
from jax.sharding import PartitionSpec as P

MESH = pl.DeviceIdType.MESH
NX, NY, NZ, NC = 4, 4, 8, 2
TOK, D, FF, TOP, CAP = 128, 1024, 384, 8, 24
PAIR = 2 * TOK
SLOTS = 2 * CAP
ROWS = NZ * SLOTS
BF = jnp.bfloat16
F32 = jnp.float32
N_SEMS = 320


def nn(a, b):
    return lax.dot_general(a, b, (((1,), (0,)), ((), ())), preferred_element_type=F32)


def nt(a, b):
    return lax.dot_general(a, b, (((1,), (1,)), ((), ())), preferred_element_type=F32)


def tn(a, b):
    return lax.dot_general(a, b, (((0,), (0,)), ((), ())), preferred_element_type=F32)


class Net:
    def __init__(self, send, recv):
        self.send_sems, self.recv_sems, self.count = send, recv, 0
        self.pending = []

    def put(self, src, dst, dev):
        n = self.count
        self.count += 1
        copy = pltpu.make_async_remote_copy(
            src_ref=src,
            dst_ref=dst,
            send_sem=self.send_sems.at[n],
            recv_sem=self.recv_sems.at[n],
            device_id=dev,
            device_id_type=MESH,
        )
        copy.start()
        self.pending.append(copy)
        return n, dev

    def got(self, ticket, dst):
        n, dev = ticket
        pltpu.make_async_remote_copy(
            src_ref=dst,
            dst_ref=dst,
            send_sem=self.send_sems.at[n],
            recv_sem=self.recv_sems.at[n],
            device_id=dev,
            device_id_type=MESH,
        ).wait_recv()

    def drain(self):
        for copy in self.pending:
            copy.wait_send()
        self.pending = []


def kernel(
    tok, grd, meta, gw, uw, dw,
    lo, tg, rg, go, uo, do,
    tok_all, grd_all, meta_all, wg, wu, wd, xs, ors, pts, w8s,
    gg, gu, gd, sib_l, sib_t, rz, rp, rr,
    r0g, r0u, r0d, r1g, r1u, r1d, r2g, r2u, r2d, hg, hu, hd,
    send_sems, recv_sems, local_sems,
):
    rep, ep = lax.axis_index("rep"), lax.axis_index("ep")
    y, c = lax.div(rep, NC), lax.rem(rep, NC)
    x, z = lax.div(ep, NZ), lax.rem(ep, NZ)

    def up_x(d):
        return lax.rem(x + d + NX, NX)

    def up_y(d):
        return lax.rem(y + d + NY, NY)

    def up_z(d):
        return lax.rem(z + d + NZ, NZ)

    def dev(dx=0, dy=0, dz=0, dc=0):
        return (
            up_y(dy) * NC + lax.rem(c + dc, NC),
            up_x(dx) * NZ + up_z(dz),
        )

    column = [(dz, dc) for dz in range(NZ) for dc in range(NC) if dz or dc]
    barrier = pltpu.get_barrier_semaphore()
    partners = [dev(dz=dz, dc=dc) for dz, dc in column]
    partners += [dev(dx=1), dev(dx=-1), dev(dy=1), dev(dy=-1)]
    for partner in partners:
        pl.semaphore_signal(barrier, inc=1, device_id=partner, device_id_type=MESH)
    pl.semaphore_wait(barrier, len(partners))

    net = Net(send_sems, recv_sems)
    sib = dev(dc=1)
    other = lax.rem(c + 1, NC)

    arrays = ((tok, tok_all), (grd, grd_all))
    last = ((4, 3), (3, 4))
    ring = {}
    sibs = {}

    def z_send(way, a, s):
        d = 1 if way == 0 else -1
        src = arrays[a][0] if s == 0 else arrays[a][1].at[up_z(-d * s), c]
        dst = arrays[a][1].at[up_z(-d * s), c]
        ring[way, a, s] = net.put(src, dst, dev(dz=d))

    def z_take(way, a, s):
        d = 1 if way == 0 else -1
        where = up_z(-d * (s + 1))
        net.got(ring[way, a, s], arrays[a][1].at[where, c])
        if s + 1 < last[way][a]:
            z_send(way, a, s + 1)
        block = arrays[a][1].at[where, c]
        sibs[a, way, s] = (net.put(block, block, sib), arrays[a][1].at[where, other])

    metas = {}
    for dz, dc in column:
        metas[dz, dc] = net.put(meta, meta_all.at[z, c], dev(dz=dz, dc=dc))
    for a in range(2):
        for way in range(2):
            z_send(way, a, 0)
    rings_x = {}

    def x_send(name, way, s, src, dst):
        rings_x[name, way, s] = net.put(src, dst, dev(dx=1 if way == 0 else -1))

    quarter = ((uw, wu), (dw, wd))
    for h in range(2):
        for m in range(2):
            for way in range(2):
                x_send((m, h), way, 0, quarter[m][0].at[c, 2 * y + h], quarter[m][1].at[x, 2 * y + h])
    for h in range(2):
        for way in range(2):
            part = pl.ds(4 * h, 4)
            x_send((2, h), way, 0, gw.at[c, part], wg.at[x, part])
    for a in range(2):
        sibs[a, 0, -1] = (
            net.put(arrays[a][0], arrays[a][1].at[z, c], sib),
            arrays[a][1].at[z, other],
        )
    local = [
        pltpu.make_async_copy(src, dst, local_sems.at[i])
        for i, (src, dst) in enumerate(
            (
                (tok, tok_all.at[z, c]),
                (grd, grd_all.at[z, c]),
                (meta, meta_all.at[z, c]),
                (gw.at[c], wg.at[x]),
                (uw.at[c], wu.at[x]),
                (dw.at[c], wd.at[x]),
            )
        )
    ]
    for copy in local:
        copy.start()

    rings_y = {}

    def y_send(name, way, s, ref):
        rings_y[name, way, s] = net.put(ref, ref, dev(dy=1 if way == 0 else -1))

    def x_take_quarters(way):
        d = 1 if way == 0 else -1
        for h in range(2):
            for m in range(2):
                piece = quarter[m][1].at[up_x(-d), 2 * y + h]
                net.got(rings_x[(m, h), way, 0], piece)
                if h == way:
                    x_send((m, h), way, 1, piece, piece)
                for to in range(2):
                    y_send((m, h, -d), to, 0, piece)

    def x_take_far():
        for m in range(2):
            for way in range(2):
                piece = quarter[m][1].at[up_x(2), 2 * y + way]
                net.got(rings_x[(m, way), way, 1], piece)
                for to in range(2):
                    y_send((m, way, 2), to, 0, piece)

    def y_take(dx):
        for m in range(2):
            for way in range(2):
                d = 1 if way == 0 else -1
                for h in range(2):
                    piece = quarter[m][1].at[up_x(dx), 2 * up_y(-d) + h]
                    net.got(rings_y[(m, h, dx), way, 0], piece)
                    if h == way:
                        y_send((m, h, dx), way, 1, piece)

    def y_take_far(dx):
        for m in range(2):
            for way in range(2):
                piece = quarter[m][1].at[up_x(dx), 2 * up_y(2) + way]
                net.got(rings_y[(m, way, dx), way, 1], piece)

    def x_take_gate():
        for way in range(2):
            d = 1 if way == 0 else -1
            for h in range(2):
                piece = wg.at[up_x(-d), pl.ds(4 * h, 4)]
                net.got(rings_x[(2, h), way, 0], piece)
                if h == way:
                    x_send((2, h), way, 1, piece, piece)

    def x_take_gate_far():
        for way in range(2):
            piece = wg.at[up_x(2), pl.ds(4 * way, 4)]
            net.got(rings_x[(2, way), way, 1], piece)

    def z_step(a, s):
        for way in range(2):
            if s < last[way][a]:
                z_take(way, a, s)

    z_step(0, 0)
    x_take_quarters(0)
    x_take_quarters(1)
    z_step(1, 0)
    x_take_far()
    z_step(0, 1)
    y_take(-1)
    z_step(1, 1)
    y_take(1)
    z_step(0, 2)
    x_take_gate()
    y_take(2)
    z_step(1, 2)
    y_take_far(-1)
    y_take_far(1)
    z_step(0, 3)
    z_step(1, 3)
    y_take_far(2)
    x_take_gate_far()
    for dz, dc in column:
        net.got(metas[dz, dc], meta_all.at[up_z(-dz), lax.rem(c + dc, NC)])
    for ticket, dst in sibs.values():
        net.got(ticket, dst)
    for copy in local:
        copy.wait()
    net.drain()

    expert_col = lax.broadcasted_iota(jnp.int32, (8, PAIR), 0)
    names = jnp.where(expert_col < NX, 2 * (expert_col * NZ + z) + c, -1).astype(F32)
    t_row = lax.broadcasted_iota(jnp.int32, (PAIR, PAIR), 0)
    t_col = lax.broadcasted_iota(jnp.int32, (PAIR, PAIR), 1)
    same = (t_row < TOK) == (t_col < TOK)
    earlier = jnp.where((t_row < t_col) & same, 1.0, 0.0).astype(BF)
    base = jnp.where(lax.broadcasted_iota(jnp.int32, (8, PAIR), 1) < TOK, 0.0, float(CAP))
    slot_no = lax.broadcasted_iota(jnp.int32, (SLOTS, PAIR), 0).astype(F32)

    def ids_of(p):
        return jnp.concatenate([meta_all[p, 0, 0:8], meta_all[p, 1, 0:8]], axis=1)

    def pack(p, carry):
        ids = ids_of(p)
        weights = jnp.concatenate([meta_all[p, 0, 8:16], meta_all[p, 1, 8:16]], axis=1)
        hot, w8 = jnp.zeros((8, PAIR), F32), jnp.zeros((8, PAIR), F32)
        for k in range(TOP):
            hit = ids[k : k + 1] == names
            hot = hot + jnp.where(hit, 1.0, 0.0)
            w8 = w8 + jnp.where(hit, weights[k : k + 1], 0.0)
        rank = nn(hot.astype(BF), earlier)
        slot = jnp.where(hot > 0.5, rank + base, -1.0)
        rows, scales = [], []
        for i in range(NX):
            one = jnp.where(slot[i : i + 1] == slot_no, 1.0, 0.0)
            rows.append(one)
            scales.append(jnp.sum(one * w8[i : i + 1], axis=1, keepdims=True))
        pt = jnp.concatenate(rows, axis=0).astype(BF)
        scale = jnp.concatenate(scales, axis=0)
        pts[p] = pt
        w8s[p] = w8
        at = pl.ds(pl.multiple_of(p * SLOTS, 16), SLOTS)
        packed = nn(pt, tok_all[p].reshape(PAIR, D)).astype(BF)
        xs[:, at, :] = packed.reshape(NX, SLOTS, D)
        scaled = (nn(pt, grd_all[p].reshape(PAIR, D)) * scale).astype(BF)
        ors[:, at, :] = scaled.reshape(NX, SLOTS, D)
        return carry

    lax.fori_loop(0, NZ, pack, 0)

    def expert(i, carry):
        gate_w, up_w = wg[i].reshape(D, FF), wu[i].reshape(D, FF)
        down_w = wd[i].reshape(FF, D)
        rows, outs = xs[i], ors[i]
        gate_pre, up_pre = nn(rows, gate_w), nn(rows, up_w)
        sig = jax.nn.sigmoid(gate_pre)
        silu = gate_pre * sig
        slope = sig * (1.0 + gate_pre * (1.0 - sig))
        hidden = (silu * up_pre).astype(BF)
        hidden_grad = nt(outs, down_w)
        gate_delta = (hidden_grad * up_pre * slope).astype(BF)
        up_delta = (hidden_grad * silu).astype(BF)
        gg[i] = tn(rows, gate_delta).astype(BF).reshape(NY, 2, D // 8, FF)
        gu[i] = tn(rows, up_delta).astype(BF).reshape(NY, 2, D // 8, FF)
        gd[i] = tn(hidden, outs).astype(BF).reshape(NY, 2, FF // 8, D)
        xs[i] = nn(hidden, down_w).astype(BF)
        ors[i] = (nt(gate_delta, gate_w) + nt(up_delta, up_w)).astype(BF)
        return carry

    lax.fori_loop(0, NX, expert, 0)

    def combine(p, carry):
        at = pl.ds(pl.multiple_of(p * SLOTS, 16), SLOTS)
        ids = ids_of(p)
        pt, w8 = pts[p].astype(F32), w8s[p]
        outs = xs[:, at, :].reshape(NX * SLOTS, D)
        ins = ors[:, at, :].reshape(NX * SLOTS, D)
        weighted = jnp.concatenate(
            [pt[i * SLOTS : (i + 1) * SLOTS] * w8[i : i + 1] for i in range(NX)], axis=0
        ).astype(BF)
        dots = nt(outs, grd_all[p].reshape(PAIR, D)) * pt
        route = jnp.zeros((8, PAIR), F32)
        for i in range(NX):
            value = jnp.sum(dots[i * SLOTS : (i + 1) * SLOTS], axis=0, keepdims=True)
            route = route + jnp.where(ids == names[i : i + 1], value, 0.0)
        rp[p, 0] = route[:, :TOK]
        rp[p, 1] = route[:, TOK:]
        tok_all[p] = tn(weighted, outs).astype(BF).reshape(2, TOK, D)
        grd_all[p] = tn(pts[p], ins).astype(BF).reshape(2, TOK, D)
        return carry

    lax.fori_loop(0, NZ, combine, 0)

    parts = (tok_all, grd_all)
    outs = (lo, tg)
    sib_bufs = (sib_l, sib_t)
    order = [4, 3, 5, 2, 6, 1, 7, 0]
    sib_tickets = {}
    for off in order:
        for a in range(2):
            sib_tickets[a, off] = net.put(
                parts[a].at[up_z(off), other], sib_bufs[a].at[up_z(off)], sib
            )
    routes = {}
    for dz, dc in column:
        routes[dz, dc] = net.put(
            rp.at[up_z(dz), lax.rem(c + dc, NC)], rr.at[z, c], dev(dz=dz, dc=dc)
        )

    grads = (gg, gu, gd)
    bufs0, bufs1, bufs2 = (r0g, r0u, r0d), (r1g, r1u, r1d), (r2g, r2u, r2d)

    def view(g, h, p, q):
        return grads[g].at[p, q, h] if h == 0 else grads[g].at[q, p, h]

    def near(h, first, d):
        along_x = (h == 0) == first
        return dev(dx=d) if along_x else dev(dy=d)

    def step(h, first, d):
        along_x = (h == 0) == first
        return up_x(d) if along_x else up_y(d)

    def add(ref, *more):
        total = ref[...].astype(F32)
        for m in more:
            total = total + m[...].astype(F32)
        ref[...] = total.astype(BF)

    tickets = {}
    half = (pl.ds(0, 2), pl.ds(2, 2))
    signs = (1, -1)
    for h in range(2):
        for way in range(2):
            for g in range(3):
                tickets[0, h, way, g] = net.put(
                    view(g, h, step(h, True, 2), half[way]),
                    bufs0[g].at[h, way],
                    near(h, True, signs[way]),
                )
    for h in range(2):
        for way in range(2):
            for g in range(3):
                free = half[1 - way]
                tickets[1, h, way, g] = net.put(
                    view(g, h, step(h, True, signs[way]), free),
                    bufs1[g].at[h, way, free],
                    near(h, True, signs[way]),
                )

    def z_part(a, off):
        net.got(sib_tickets[a, off], sib_bufs[a].at[up_z(off)])

    chain = {}
    buf_no = {}
    for way in range(2):
        for a in range(2):
            for s in range(last[way][a]):
                buf_no[way, a, s] = len(buf_no)

    def z_pass(way, a, s):
        d = signs[way]
        off = d * (last[way][a] - s)
        z_part(a, off % NZ)
        block = parts[a].at[up_z(off), c]
        more = [sib_bufs[a].at[up_z(off)]]
        if s > 0:
            came = rz.at[buf_no[way, a, s - 1]]
            net.got(chain[way, a, s - 1], came)
            more.append(came)
        add(block, *more)
        chain[way, a, s] = net.put(block, rz.at[buf_no[way, a, s]], dev(dz=d))

    def grad_second(h):
        for way in range(2):
            for g in range(3):
                net.got(tickets[0, h, way, g], bufs0[g].at[h, way])
                mine = view(g, h, step(h, True, signs[way]), half[way])
                add(mine, bufs0[g].at[h, way])
                tickets[2, h, way, g] = net.put(
                    mine, bufs1[g].at[h, way, half[way]], near(h, True, signs[way])
                )

    far_way = ((0, 1, 0), (0, 1, 1))

    def grad_third(h):
        me = step(h, True, 0)
        for g in range(3):
            for way in range(2):
                net.got(tickets[1, h, way, g], bufs1[g].at[h, way, half[1 - way]])
                net.got(tickets[2, h, way, g], bufs1[g].at[h, way, half[way]])
            mine = view(g, h, me, pl.ds(0, 4))
            add(mine, bufs1[g].at[h, 0], bufs1[g].at[h, 1])
            way = far_way[h][g]
            tickets[3, h, g] = net.put(
                view(g, h, me, step(h, False, 2)),
                bufs2[g].at[h, 2],
                near(h, False, signs[way]),
            )
            tickets[4, h, g] = net.put(
                view(g, h, me, step(h, False, signs[1 - way])),
                bufs2[g].at[h, 1 - way],
                near(h, False, signs[1 - way]),
            )

    def grad_fourth(h):
        me = step(h, True, 0)
        for g in range(3):
            way = far_way[h][g]
            net.got(tickets[3, h, g], bufs2[g].at[h, 2])
            mine = view(g, h, me, step(h, False, signs[way]))
            add(mine, bufs2[g].at[h, 2])
            tickets[5, h, g] = net.put(
                mine, bufs2[g].at[h, way], near(h, False, signs[way])
            )

    for way in range(2):
        for a in range(2):
            if last[way][a] == 4:
                z_pass(way, a, 0)
    for way in range(2):
        for a in range(2):
            z_pass(way, a, last[way][a] - 3)
    grad_second(0)
    grad_second(1)
    for n in (2, 1):
        for way in range(2):
            for a in range(2):
                z_pass(way, a, last[way][a] - n)
    grad_third(0)
    grad_third(1)
    for a in range(2):
        z_part(a, 0)
        total = parts[a][z, c].astype(F32) + sib_bufs[a][z].astype(F32)
        for way in range(2):
            s = last[way][a] - 1
            came = rz.at[buf_no[way, a, s]]
            net.got(chain[way, a, s], came)
            total = total + came[...].astype(F32)
        outs[a][...] = total.astype(BF)
    total = rp[z, c]
    for dz, dc in column:
        came = rr.at[up_z(-dz), lax.rem(c + dc, NC)]
        net.got(routes[dz, dc], came)
        total = total + came[...]
    rg[...] = total
    grad_fourth(0)
    grad_fourth(1)

    finals = (go, uo, do)
    for h in range(2):
        for g in range(3):
            way = far_way[h][g]
            net.got(tickets[4, h, g], bufs2[g].at[h, 1 - way])
            net.got(tickets[5, h, g], bufs2[g].at[h, way])
    stage = (hg, hu, hd)
    hand = []
    for g in range(3):

        def whole(h):
            me = view(g, h, step(h, True, 0), step(h, False, 0))
            return (
                me[...].astype(F32)
                + bufs2[g][h, 0].astype(F32)
                + bufs2[g][h, 1].astype(F32)
            )

        both = (whole(0), whole(1))
        finals[g][c] = jnp.where(c == 0, both[0], both[1])
        away = jnp.where(c == 0, both[1], both[0])
        stage[g][0] = away.astype(BF)
        hand.append(net.put(stage[g].at[0], stage[g].at[1], sib))
    for g in range(3):
        net.got(hand[g], stage[g].at[1])
        finals[g][other] = stage[g][1].astype(F32)
    net.drain()


def per_device(tokens, expert_ids, route_weights, out_grad, gate_weight, up_weight, down_weight):
    meta = jnp.concatenate([expert_ids.astype(F32).T, route_weights.T], axis=0)
    gate_weight = gate_weight.reshape(2, 8, D // 8, FF)
    up_weight = up_weight.reshape(2, 8, D // 8, FF)
    down_weight = down_weight.reshape(2, 8, FF // 8, D)
    vmem = pl.BlockSpec(memory_space=pltpu.VMEM)
    hbm = pl.BlockSpec(memory_space=pl.ANY)
    wide, tall = (D // 8, FF), (FF // 8, D)
    piece = (wide, wide, tall)
    layer_out, token_grad, route_grad, gate_share, up_share, down_share = pl.pallas_call(
        kernel,
        out_shape=(
            jax.ShapeDtypeStruct((TOK, D), BF),
            jax.ShapeDtypeStruct((TOK, D), BF),
            jax.ShapeDtypeStruct((TOP, TOK), F32),
            jax.ShapeDtypeStruct((2, *wide), F32),
            jax.ShapeDtypeStruct((2, *wide), F32),
            jax.ShapeDtypeStruct((2, *tall), F32),
        ),
        in_specs=[vmem, vmem, vmem, hbm, hbm, hbm],
        out_specs=(vmem,) * 6,
        scratch_shapes=[
            pltpu.VMEM((NZ, NC, TOK, D), BF),
            pltpu.VMEM((NZ, NC, TOK, D), BF),
            pltpu.VMEM((NZ, NC, 16, TOK), F32),
            pltpu.VMEM((NX, 8, *wide), BF),
            pltpu.VMEM((NX, 8, *wide), BF),
            pltpu.VMEM((NX, 8, *tall), BF),
            pltpu.VMEM((NX, ROWS, D), BF),
            pltpu.VMEM((NX, ROWS, D), BF),
            pltpu.VMEM((NZ, NX * SLOTS, PAIR), BF),
            pltpu.VMEM((NZ, 8, PAIR), F32),
            pltpu.VMEM((NX, NY, 2, *wide), BF),
            pltpu.VMEM((NX, NY, 2, *wide), BF),
            pltpu.VMEM((NX, NY, 2, *tall), BF),
            pltpu.VMEM((NZ, TOK, D), BF),
            pltpu.VMEM((NZ, TOK, D), BF),
            pltpu.VMEM((14, TOK, D), BF),
            pltpu.VMEM((NZ, NC, TOP, TOK), F32),
            pltpu.VMEM((NZ, NC, TOP, TOK), F32),
            *[pltpu.VMEM((2, 2, 2, *s), BF) for s in piece],
            *[pltpu.VMEM((2, 2, 4, *s), BF) for s in piece],
            *[pltpu.VMEM((2, 3, *s), BF) for s in piece],
            *[pltpu.VMEM((2, *s), BF) for s in piece],
            pltpu.SemaphoreType.DMA((N_SEMS,)),
            pltpu.SemaphoreType.DMA((N_SEMS,)),
            pltpu.SemaphoreType.DMA((6,)),
        ],
        compiler_params=pltpu.CompilerParams(
            collective_id=0,
            has_side_effects=True,
            vmem_limit_bytes=62 * 1024 * 1024,
        ),
    )(tokens, out_grad, meta, gate_weight, up_weight, down_weight)
    return (layer_out, token_grad, route_grad.T, gate_share, up_share, down_share)


def solution(mesh):
    return jax.shard_map(
        per_device,
        mesh=mesh,
        in_specs=(
            P(("rep", "ep"), None),
            P(("rep", "ep"), None),
            P(("rep", "ep"), None),
            P(("rep", "ep"), None),
            P("ep", None, None),
            P("ep", None, None),
            P("ep", None, None),
        ),
        out_specs=(
            P(("rep", "ep"), None),
            P(("rep", "ep"), None),
            P(("rep", "ep"), None),
            P("ep", "rep", None),
            P("ep", "rep", None),
            P("ep", "rep", None),
        ),
        check_vma=False,
    )
```

```python
import jax
import jax.numpy as jnp
from jax import lax
from jax.experimental import pallas as pl
from jax.experimental.pallas import tpu as pltpu
from jax.sharding import PartitionSpec as P

MESH = pl.DeviceIdType.MESH
NX, NY, NZ, NC = 4, 4, 8, 2
TOK, D, FF, TOP, CAP = 128, 1024, 384, 8, 24
PAIR = 2 * TOK
SLOTS = 2 * CAP
ROWS = NZ * SLOTS
BF = jnp.bfloat16
F32 = jnp.float32


def nn(a, b):
    return lax.dot_general(a, b, (((1,), (0,)), ((), ())), preferred_element_type=F32)


def nt(a, b):
    return lax.dot_general(a, b, (((1,), (1,)), ((), ())), preferred_element_type=F32)


def tn(a, b):
    return lax.dot_general(a, b, (((0,), (0,)), ((), ())), preferred_element_type=F32)


class Net:
    def __init__(self, send, recv):
        self.send_sems, self.recv_sems = send, recv
        self.sent = self.count = 0
        self.pending = []

    def copy(self, src, dst, dev, out, into):
        return pltpu.make_async_remote_copy(
            src_ref=src,
            dst_ref=dst,
            send_sem=self.send_sems.at[out],
            recv_sem=self.recv_sems.at[into],
            device_id=dev,
            device_id_type=MESH,
        )

    def put(self, src, dst, dev):
        copy = self.copy(src, dst, dev, self.sent, self.count)
        copy.start()
        self.pending.append(copy)
        self.sent, self.count = self.sent + 1, self.count + 1
        return self.count - 1, dev

    def got(self, ticket, dst):
        into, dev = ticket
        self.copy(dst, dst, dev, 0, into).wait_recv()

    def drain(self):
        for copy in self.pending:
            copy.wait_send()
        self.pending, self.sent = [], 0


N_SEND, N_RECV = 110, 210
SIGNS = (1, -1)
LAST = ((4, 3), (3, 4))


def kernel(
    tok, grd, ids_in, weights_in, gw, uw, dw,
    lo, tg, rg, go, uo, do,
    tok_all, grd_all, meta_all, wg, wu, wd, xs, ors, igs, pts, w8s,
    gx, gd, sib_l, sib_t, sib_r, rz, zr, rp,
    xfx, xfd, xnx, xnd, yfx, yfd, ynx, ynd, sx, sd, hx, hd,
    send_sems, recv_sems, local_sems,
):
    rep, ep = lax.axis_index("rep"), lax.axis_index("ep")
    y, c = lax.div(rep, NC), lax.rem(rep, NC)
    x, z = lax.div(ep, NZ), lax.rem(ep, NZ)

    def up_x(d):
        return lax.rem(x + d + NX, NX)

    def up_y(d):
        return lax.rem(y + d + NY, NY)

    def up_z(d):
        return lax.rem(z + d + NZ, NZ)

    def dev(dx=0, dy=0, dz=0, dc=0):
        return (
            up_y(dy) * NC + lax.rem(c + dc, NC),
            up_x(dx) * NZ + up_z(dz),
        )

    sib = dev(dc=1)
    other = lax.rem(c + 1, NC)
    barrier = pltpu.get_barrier_semaphore()
    partners = [sib, dev(dx=1), dev(dx=-1), dev(dy=1), dev(dy=-1), dev(dz=1), dev(dz=-1)]
    for partner in partners:
        pl.semaphore_signal(barrier, inc=1, device_id=partner, device_id_type=MESH)
    meta_all[z, c, 0:8] = ids_in[...].astype(F32)
    meta_all[z, c, 8:16] = weights_in[...]
    pl.semaphore_wait(barrier, len(partners))
    net = Net(send_sems, recv_sems)

    blocks = (tok_all, grd_all)
    firsts = (tok, grd)
    ring, sibs = {}, {}

    def z_send(way, a, s):
        d = SIGNS[way]
        block = blocks[a].at[up_z(-d * s), c]
        src = firsts[a] if s == 0 else block
        ring[way, a, s] = net.put(src, block, dev(dz=d))
        if a == 0:
            note = meta_all.at[up_z(-d * s), c]
            ring[way, 2, s] = net.put(note, note, dev(dz=d))

    def z_step(a, s):
        for way in range(2):
            if s < LAST[way][a]:
                off = -SIGNS[way] * (s + 1)
                where = up_z(off)
                block = blocks[a].at[where, c]
                net.got(ring[way, a, s], block)
                if a == 0:
                    net.got(ring[way, 2, s], meta_all.at[where, c])
                if s + 1 < LAST[way][a]:
                    z_send(way, a, s + 1)
                share(a, off, block)

    def share(a, off, src):
        where = up_z(off)
        sibs[a, off % NZ] = net.put(src, blocks[a].at[where, c], sib)
        if a == 0:
            note = meta_all.at[where, c]
            sibs[2, off % NZ] = net.put(note, note, sib)

    for a in range(2):
        for way in range(2):
            z_send(way, a, 0)
    rings_x = {}

    def x_send(name, way, s, src, dst):
        rings_x[name, way, s] = net.put(src, dst, dev(dx=SIGNS[way]))

    quarter = ((uw, wu), (dw, wd))
    for h in range(2):
        for m in range(2):
            for way in range(2):
                x_send((m, h), way, 0, quarter[m][0].at[c, 2 * y + h], quarter[m][1].at[x, 2 * y + h])
    for h in range(2):
        for way in range(2):
            part = pl.ds(4 * h, 4)
            x_send((2, h), way, 0, gw.at[c, part], wg.at[x, part])
    for a in range(2):
        share(a, 0, firsts[a])
    local = [
        pltpu.make_async_copy(src, dst, local_sems.at[i])
        for i, (src, dst) in enumerate(
            (
                (tok, tok_all.at[z, c]),
                (grd, grd_all.at[z, c]),
                (gw.at[c], wg.at[x]),
                (uw.at[c], wu.at[x]),
                (dw.at[c], wd.at[x]),
            )
        )
    ]
    for copy in local:
        copy.start()

    rings_y = {}

    def y_send(name, way, s, ref):
        rings_y[name, way, s] = net.put(ref, ref, dev(dy=SIGNS[way]))

    def x_take_quarters(way):
        d = SIGNS[way]
        for h in range(2):
            for m in range(2):
                piece = quarter[m][1].at[up_x(-d), 2 * y + h]
                net.got(rings_x[(m, h), way, 0], piece)
                if h == way:
                    x_send((m, h), way, 1, piece, piece)
                for to in range(2):
                    y_send((m, h, -d), to, 0, piece)

    def x_take_far():
        for m in range(2):
            for way in range(2):
                piece = quarter[m][1].at[up_x(2), 2 * y + way]
                net.got(rings_x[(m, way), way, 1], piece)
                for to in range(2):
                    y_send((m, way, 2), to, 0, piece)

    def y_take(dx):
        for m in range(2):
            for way in range(2):
                for h in range(2):
                    piece = quarter[m][1].at[up_x(dx), 2 * up_y(-SIGNS[way]) + h]
                    net.got(rings_y[(m, h, dx), way, 0], piece)
                    if h == way:
                        y_send((m, h, dx), way, 1, piece)

    def y_take_far(dx):
        for m in range(2):
            for way in range(2):
                piece = quarter[m][1].at[up_x(dx), 2 * up_y(2) + way]
                net.got(rings_y[(m, way, dx), way, 1], piece)

    def x_take_gate():
        for way in range(2):
            for h in range(2):
                piece = wg.at[up_x(-SIGNS[way]), pl.ds(4 * h, 4)]
                net.got(rings_x[(2, h), way, 0], piece)
                if h == way:
                    x_send((2, h), way, 1, piece, piece)

    def x_take_gate_far():
        for way in range(2):
            piece = wg.at[up_x(2), pl.ds(4 * way, 4)]
            net.got(rings_x[(2, way), way, 1], piece)

    expert_col = lax.broadcasted_iota(jnp.int32, (8, PAIR), 0)
    names = jnp.where(expert_col < NX, 2 * (expert_col * NZ + z) + c, -1).astype(F32)
    t_row = lax.broadcasted_iota(jnp.int32, (PAIR, PAIR), 0)
    t_col = lax.broadcasted_iota(jnp.int32, (PAIR, PAIR), 1)
    same = (t_row < TOK) == (t_col < TOK)
    earlier = jnp.where((t_row < t_col) & same, 1.0, 0.0).astype(BF)
    base = jnp.where(lax.broadcasted_iota(jnp.int32, (8, PAIR), 1) < TOK, 0.0, float(CAP))
    slot_no = lax.broadcasted_iota(jnp.int32, (SLOTS, PAIR), 0).astype(F32)

    def ids_of(p):
        return jnp.concatenate([meta_all[p, 0, 0:8], meta_all[p, 1, 0:8]], axis=1)

    def pack(off):
        p = up_z(off)
        for a in range(2):
            net.got(sibs[a, off % NZ], blocks[a].at[p, other])
        net.got(sibs[2, off % NZ], meta_all.at[p, other])
        ids = ids_of(p)
        weights = jnp.concatenate([meta_all[p, 0, 8:16], meta_all[p, 1, 8:16]], axis=1)
        hot, w8 = jnp.zeros((8, PAIR), F32), jnp.zeros((8, PAIR), F32)
        for k in range(TOP):
            hit = ids[k : k + 1] == names
            hot = hot + jnp.where(hit, 1.0, 0.0)
            w8 = w8 + jnp.where(hit, weights[k : k + 1], 0.0)
        rank = nn(hot.astype(BF), earlier)
        slot = jnp.where(hot > 0.5, rank + base, -1.0)
        rows, scales = [], []
        for i in range(NX):
            one = jnp.where(slot[i : i + 1] == slot_no, 1.0, 0.0)
            rows.append(one)
            scales.append(jnp.sum(one * w8[i : i + 1], axis=1, keepdims=True))
        pt = jnp.concatenate(rows, axis=0).astype(BF)
        scale = jnp.concatenate(scales, axis=0)
        pts[p] = pt
        w8s[p] = w8
        at = pl.ds(pl.multiple_of(p * SLOTS, 16), SLOTS)
        packed = nn(pt, tok_all[p].reshape(PAIR, D)).astype(BF)
        xs[:, at, :] = packed.reshape(NX, SLOTS, D)
        scaled = (nn(pt, grd_all[p].reshape(PAIR, D)) * scale).astype(BF)
        ors[:, at, :] = scaled.reshape(NX, SLOTS, D)

    def expert(dx):
        i = up_x(dx)
        gate_w, up_w = wg[i].reshape(D, FF), wu[i].reshape(D, FF)
        down_w = wd[i].reshape(FF, D)
        rows, outs = xs[i], ors[i]
        gate_pre, up_pre = nn(rows, gate_w), nn(rows, up_w)
        sig = jax.nn.sigmoid(gate_pre)
        silu = gate_pre * sig
        slope = sig * (1.0 + gate_pre * (1.0 - sig))
        hidden = (silu * up_pre).astype(BF)
        hidden_grad = nt(outs, down_w)
        gate_delta = (hidden_grad * up_pre * slope).astype(BF)
        up_delta = (hidden_grad * silu).astype(BF)
        igs[i] = (nt(gate_delta, gate_w) + nt(up_delta, up_w)).astype(BF)
        expert_out = nn(hidden, down_w).astype(BF)
        wd[i] = expert_out.reshape(8, ROWS // 8, D)
        wg[i, 0:3] = hidden.reshape(3, TOK, FF)
        wu[i, 0:3] = gate_delta.reshape(3, TOK, FF)
        wu[i, 3:6] = up_delta.reshape(3, TOK, FF)

    def weight_grads(dx):
        i = up_x(dx)
        rows, outs = xs[i], ors[i]
        for m in range(2):
            delta = wu[i, 3 * m : 3 * m + 3].reshape(ROWS, FF)
            gx[i, :, :, m] = tn(rows, delta).astype(BF).reshape(NY, 2, TOK, FF)
        hidden = wg[i, 0:3].reshape(ROWS, FF)
        gd[i] = tn(hidden, outs).astype(BF).reshape(NY, 2, FF // 8, D)

    parts = (tok_all, grd_all)
    sib_bufs = (sib_l, sib_t)
    sib_tickets = {}

    def combine(off):
        p = up_z(off)
        ids = ids_of(p)
        pt, w8 = pts[p].astype(F32), w8s[p]
        outs = wd[:, p].reshape(NX * SLOTS, D)
        at = pl.ds(pl.multiple_of(p * SLOTS, 16), SLOTS)
        ins = igs[:, at, :].reshape(NX * SLOTS, D)
        weighted = jnp.concatenate(
            [pt[i * SLOTS : (i + 1) * SLOTS] * w8[i : i + 1] for i in range(NX)], axis=0
        ).astype(BF)
        dots = nt(outs, grd_all[p].reshape(PAIR, D)) * pt
        route = jnp.zeros((8, PAIR), F32)
        for i in range(NX):
            value = jnp.sum(dots[i * SLOTS : (i + 1) * SLOTS], axis=0, keepdims=True)
            route = route + jnp.where(ids == names[i : i + 1], value, 0.0)
        rp[p, 0] = route[:, :TOK]
        rp[p, 1] = route[:, TOK:]
        tok_all[p] = tn(weighted, outs).astype(BF).reshape(2, TOK, D)
        grd_all[p] = tn(pts[p], ins).astype(BF).reshape(2, TOK, D)
        for a in range(2):
            sib_tickets[a, off % NZ] = net.put(parts[a].at[p, other], sib_bufs[a].at[p], sib)
        sib_tickets[2, off % NZ] = net.put(rp.at[p, other], sib_r.at[p], sib)

    z_step(0, 0)
    x_take_quarters(0)
    x_take_quarters(1)
    for copy in local:
        copy.wait()
    z_step(1, 0)
    x_take_far()
    pack(0)
    z_step(0, 1)
    y_take(-1)
    pack(1)
    pack(-1)
    z_step(1, 1)
    y_take(1)
    z_step(0, 2)
    x_take_gate()
    y_take(2)
    pack(2)
    pack(-2)
    z_step(1, 2)
    y_take_far(-1)
    y_take_far(1)
    z_step(0, 3)
    pack(3)
    pack(-3)
    z_step(1, 3)
    y_take_far(2)
    x_take_gate_far()
    pack(4)
    net.drain()

    grads = (gx, gd)
    chain, tickets = {}, {}
    buf_no = {}
    for way in range(2):
        for a in range(2):
            for s in range(LAST[way][a]):
                buf_no[way, a, s] = len(buf_no)

    def add(ref, *more):
        total = ref[...].astype(F32)
        for m in more:
            total = total + m[...].astype(F32)
        ref[...] = total.astype(BF)

    def z_pass(way, a, s):
        d = SIGNS[way]
        off = d * (LAST[way][a] - s)
        where = up_z(off)
        net.got(sib_tickets[a, off % NZ], sib_bufs[a].at[where])
        block = parts[a].at[where, c]
        more = [sib_bufs[a].at[where]]
        if s > 0:
            came = rz.at[buf_no[way, a, s - 1]]
            net.got(chain[way, a, s - 1], came)
            more.append(came)
        add(block, *more)
        chain[way, a, s] = net.put(block, rz.at[buf_no[way, a, s]], dev(dz=d))
        if a == 0:
            net.got(sib_tickets[2, off % NZ], sib_r.at[where])
            route = rp[where, c] + sib_r[where]
            if s > 0:
                net.got(chain[way, 2, s - 1], zr.at[buf_no[way, 0, s - 1]])
                route = route + zr[buf_no[way, 0, s - 1]]
            rp[where, c] = route
            chain[way, 2, s] = net.put(
                rp.at[where, c], zr.at[buf_no[way, 0, s]], dev(dz=d)
            )

    half = (pl.ds(0, 2), pl.ds(2, 2))
    far_x, near_x = (xfx, xfd), (xnx, xnd)
    far_y, near_y = (yfx, yfd), (ynx, ynd)
    second = (sx, sd)

    def y_way(dx):
        return 0 if dx in (2, 1) else 1

    def grad_send(dx):
        i = up_x(dx)
        for g in range(2):
            if dx == 2:
                for way in range(2):
                    tickets["xf", way, g] = net.put(
                        grads[g].at[i, half[way], 0], far_x[g].at[way], dev(dx=SIGNS[way])
                    )
            elif dx:
                way = SIGNS.index(dx)
                free = half[1 - way]
                tickets["xa", way, g] = net.put(
                    grads[g].at[i, free, 0], near_x[g].at[way, free], dev(dx=dx)
                )
            way = y_way(dx)
            tickets["yf", dx, g] = net.put(
                grads[g].at[i, up_y(2), 1], far_y[g].at[dx % NX], dev(dy=SIGNS[way])
            )
            tickets["yn", dx, 1 - way, g] = net.put(
                grads[g].at[i, up_y(SIGNS[1 - way]), 1],
                near_y[g].at[dx % NX, 1 - way],
                dev(dy=SIGNS[1 - way]),
            )

    def x_pass(way):
        i = up_x(SIGNS[way])
        for g in range(2):
            net.got(tickets["xf", way, g], far_x[g].at[way])
            mine = grads[g].at[i, half[way], 0]
            add(mine, far_x[g].at[way])
            tickets["xb", way, g] = net.put(
                mine, near_x[g].at[way, half[way]], dev(dx=SIGNS[way])
            )

    def y_pass(dx):
        way = y_way(dx)
        for g in range(2):
            net.got(tickets["yf", dx, g], far_y[g].at[dx % NX])
            mine = grads[g].at[up_x(dx), up_y(SIGNS[way]), 1]
            add(mine, far_y[g].at[dx % NX])
            tickets["yn", dx, way, g] = net.put(
                mine, near_y[g].at[dx % NX, way], dev(dy=SIGNS[way])
            )

    def second_view(h, g, d):
        return grads[g].at[x, up_y(d), 0] if h == 0 else grads[g].at[up_x(d), y, 1]

    def second_dev(h, way):
        return dev(dy=SIGNS[way]) if h == 0 else dev(dx=SIGNS[way])

    def second_send(h, g):
        way = g
        tickets["sf", h, g] = net.put(
            second_view(h, g, 2), second[g].at[h, 2], second_dev(h, way)
        )
        tickets["sn", h, g, 1 - way] = net.put(
            second_view(h, g, SIGNS[1 - way]), second[g].at[h, 1 - way], second_dev(h, 1 - way)
        )

    def x_last():
        for g in range(2):
            for way in range(2):
                net.got(tickets["xa", way, g], near_x[g].at[way, half[1 - way]])
                net.got(tickets["xb", way, g], near_x[g].at[way, half[way]])
            add(grads[g].at[x, :, 0], near_x[g].at[0], near_x[g].at[1])
            second_send(0, g)

    def y_last():
        for g in range(2):
            for dx in (2, 1, -1, 0):
                for way in range(2):
                    net.got(tickets["yn", dx, way, g], near_y[g].at[dx % NX, way])
                near = near_y[g].at[dx % NX]
                add(grads[g].at[up_x(dx), y, 1], near.at[0], near.at[1])
            second_send(1, g)

    def second_pass(h):
        for g in range(2):
            way = g
            net.got(tickets["sf", h, g], second[g].at[h, 2])
            mine = second_view(h, g, SIGNS[way])
            add(mine, second[g].at[h, 2])
            tickets["sn", h, g, way] = net.put(
                mine, second[g].at[h, way], second_dev(h, way)
            )

    expert(2)
    weight_grads(2)
    grad_send(2)
    expert(1)
    expert(-1)
    expert(0)
    combine(4)
    combine(3)
    combine(-3)
    z_pass(0, 0, 0)
    z_pass(1, 1, 0)
    z_pass(0, 1, 0)
    z_pass(1, 0, 0)
    weight_grads(1)
    grad_send(1)
    weight_grads(-1)
    grad_send(-1)
    x_pass(0)
    x_pass(1)
    combine(2)
    combine(-2)
    z_pass(0, 0, 1)
    z_pass(1, 1, 1)
    weight_grads(0)
    grad_send(0)
    z_pass(0, 1, 1)
    z_pass(1, 0, 1)
    y_pass(2)
    y_pass(1)
    y_pass(-1)
    combine(1)
    combine(-1)
    z_pass(0, 0, 2)
    z_pass(1, 1, 2)
    y_pass(0)
    x_last()
    z_pass(0, 1, 2)
    z_pass(1, 0, 2)
    combine(0)
    y_last()
    z_pass(0, 0, 3)
    z_pass(1, 1, 3)
    second_pass(0)
    second_pass(1)

    results = (lo, tg)
    for a in range(2):
        net.got(sib_tickets[a, 0], sib_bufs[a].at[z])
        total = parts[a][z, c].astype(F32) + sib_bufs[a][z].astype(F32)
        for way in range(2):
            s = LAST[way][a] - 1
            came = rz.at[buf_no[way, a, s]]
            net.got(chain[way, a, s], came)
            total = total + came[...].astype(F32)
        results[a][...] = total.astype(BF)
    net.got(sib_tickets[2, 0], sib_r.at[z])
    total = rp[z, c] + sib_r[z]
    for way in range(2):
        no = buf_no[way, 0, LAST[way][0] - 1]
        net.got(chain[way, 2, LAST[way][0] - 1], zr.at[no])
        total = total + zr[no]
    rg[...] = total

    finals = ((go, uo), (do,))
    stage = (hx, hd)
    hand = []
    for g in range(2):
        both = []
        for h in range(2):
            for way in range(2):
                net.got(tickets["sn", h, g, way], second[g].at[h, way])
            both.append(
                second_view(h, g, 0)[...].astype(F32)
                + second[g][h, 0].astype(F32)
                + second[g][h, 1].astype(F32)
            )
        keep = jnp.where(c == 0, both[0], both[1])
        away = jnp.where(c == 0, both[1], both[0])
        stage[g][0] = away.astype(BF)
        hand.append(net.put(stage[g].at[0], stage[g].at[1], sib))
        if g == 0:
            go[c], uo[c] = keep[0], keep[1]
        else:
            do[c] = keep
    net.got(hand[0], hx.at[1])
    go[other] = hx[1, 0].astype(F32)
    uo[other] = hx[1, 1].astype(F32)
    net.got(hand[1], hd.at[1])
    do[other] = hd[1].astype(F32)
    net.drain()


def hand_out(*refs):
    n = len(refs) // 2
    copies = [
        pltpu.make_async_copy(refs[i], refs[n + i], refs[2 * n].at[i]) for i in range(n)
    ]
    for copy in copies:
        copy.start()
    for copy in copies:
        copy.wait()


def per_device(tokens, expert_ids, route_weights, out_grad, gate_weight, up_weight, down_weight):
    gate_weight = gate_weight.reshape(2, 8, D // 8, FF)
    up_weight = up_weight.reshape(2, 8, D // 8, FF)
    down_weight = down_weight.reshape(2, 8, FF // 8, D)
    vmem = pl.BlockSpec(memory_space=pltpu.VMEM)
    hbm = pl.BlockSpec(memory_space=pl.ANY)
    wide, tall = (D // 8, FF), (FF // 8, D)
    two = (2, *wide)
    out_shape = (
        jax.ShapeDtypeStruct((TOK, D), BF),
        jax.ShapeDtypeStruct((TOK, D), BF),
        jax.ShapeDtypeStruct((TOP, TOK), F32),
        jax.ShapeDtypeStruct((2, *wide), F32),
        jax.ShapeDtypeStruct((2, *wide), F32),
        jax.ShapeDtypeStruct((2, *tall), F32),
    )
    results = pl.pallas_call(
        kernel,
        out_shape=out_shape,
        in_specs=[vmem, vmem, vmem, vmem, hbm, hbm, hbm],
        out_specs=(vmem,) * 6,
        scratch_shapes=[
            pltpu.VMEM((NZ, NC, TOK, D), BF),
            pltpu.VMEM((NZ, NC, TOK, D), BF),
            pltpu.VMEM((NZ, NC, 16, TOK), F32),
            pltpu.VMEM((NX, 8, *wide), BF),
            pltpu.VMEM((NX, 8, *wide), BF),
            pltpu.VMEM((NX, 8, *tall), BF),
            pltpu.VMEM((NX, ROWS, D), BF),
            pltpu.VMEM((NX, ROWS, D), BF),
            pltpu.VMEM((NX, ROWS, D), BF),
            pltpu.VMEM((NZ, NX * SLOTS, PAIR), BF),
            pltpu.VMEM((NZ, 8, PAIR), F32),
            pltpu.VMEM((NX, NY, 2, *two), BF),
            pltpu.VMEM((NX, NY, 2, *tall), BF),
            pltpu.VMEM((NZ, TOK, D), BF),
            pltpu.VMEM((NZ, TOK, D), BF),
            pltpu.VMEM((NZ, TOP, TOK), F32),
            pltpu.VMEM((14, TOK, D), BF),
            pltpu.VMEM((14, TOP, TOK), F32),
            pltpu.VMEM((NZ, NC, TOP, TOK), F32),
            *[pltpu.VMEM((2, 2, *s), BF) for s in (two, tall)],
            *[pltpu.VMEM((2, 4, *s), BF) for s in (two, tall)],
            *[pltpu.VMEM((4, *s), BF) for s in (two, tall)],
            *[pltpu.VMEM((4, 2, *s), BF) for s in (two, tall)],
            *[pltpu.VMEM((2, 3, *s), BF) for s in (two, tall)],
            *[pltpu.VMEM((2, *s), BF) for s in (two, tall)],
            pltpu.SemaphoreType.DMA((N_SEND,)),
            pltpu.SemaphoreType.DMA((N_RECV,)),
            pltpu.SemaphoreType.DMA((5,)),
        ],
        compiler_params=pltpu.CompilerParams(
            collective_id=0,
            has_side_effects=True,
            vmem_limit_bytes=63 * 1024 * 1024,
        ),
    )(tokens, out_grad, expert_ids.T, route_weights.T, gate_weight, up_weight, down_weight)
    layer_out, token_grad, route_grad, gate_share, up_share, down_share = pl.pallas_call(
        hand_out,
        out_shape=out_shape,
        in_specs=[hbm] * 6,
        out_specs=(hbm,) * 6,
        scratch_shapes=[pltpu.SemaphoreType.DMA((6,))],
    )(*results)
    return (layer_out, token_grad, route_grad.T, gate_share, up_share, down_share)


def solution(mesh):
    return jax.shard_map(
        per_device,
        mesh=mesh,
        in_specs=(
            P(("rep", "ep"), None),
            P(("rep", "ep"), None),
            P(("rep", "ep"), None),
            P(("rep", "ep"), None),
            P("ep", None, None),
            P("ep", None, None),
            P("ep", None, None),
        ),
        out_specs=(
            P(("rep", "ep"), None),
            P(("rep", "ep"), None),
            P(("rep", "ep"), None),
            P("ep", "rep", None),
            P("ep", "rep", None),
            P("ep", "rep", None),
        ),
        check_vma=False,
    )
```

```python
import jax
import jax.numpy as jnp
from jax import lax
from jax.experimental import pallas as pl
from jax.experimental.pallas import tpu as pltpu
from jax.sharding import PartitionSpec as P

MESH = pl.DeviceIdType.MESH
NX, NY, NZ, NC = 4, 4, 8, 2
TOK, D, FF, TOP, CAP = 128, 1024, 384, 8, 24
PAIR = 2 * TOK
SLOTS = 2 * CAP
ROWS = NZ * SLOTS
BF = jnp.bfloat16
F32 = jnp.float32


def nn(a, b):
    return lax.dot_general(a, b, (((1,), (0,)), ((), ())), preferred_element_type=F32)


def nt(a, b):
    return lax.dot_general(a, b, (((1,), (1,)), ((), ())), preferred_element_type=F32)


def tn(a, b):
    return lax.dot_general(a, b, (((0,), (0,)), ((), ())), preferred_element_type=F32)


class Net:
    def __init__(self, send, recv):
        self.send_sems, self.recv_sems = send, recv
        self.sent = self.count = 0
        self.pending = []

    def copy(self, src, dst, dev, out, into):
        return pltpu.make_async_remote_copy(
            src_ref=src,
            dst_ref=dst,
            send_sem=self.send_sems.at[out],
            recv_sem=self.recv_sems.at[into],
            device_id=dev,
            device_id_type=MESH,
        )

    def put(self, src, dst, dev):
        copy = self.copy(src, dst, dev, self.sent, self.count)
        copy.start()
        self.pending.append(copy)
        self.sent, self.count = self.sent + 1, self.count + 1
        return self.count - 1, dev

    def got(self, ticket, dst):
        into, dev = ticket
        self.copy(dst, dst, dev, 0, into).wait_recv()

    def drain(self):
        for copy in self.pending:
            copy.wait_send()
        self.pending, self.sent = [], 0


N_SEND, N_RECV = 110, 210
SIGNS = (1, -1)
LAST = ((4, 3), (3, 4))


def kernel(
    tok, grd, ids_in, weights_in, gw, uw, dw,
    lo, tg, rg, go, uo, do,
    tok_all, grd_all, meta_all, wg, wu, wd, xs, ors, igs, pts, w8s,
    gx, gd, sib_l, sib_t, sib_r, rz, zr, rp,
    xfx, xfd, xnx, xnd, yfx, yfd, ynx, ynd, sx, sd, hx, hd,
    send_sems, recv_sems, local_sems,
):
    rep, ep = lax.axis_index("rep"), lax.axis_index("ep")
    y, c = lax.div(rep, NC), lax.rem(rep, NC)
    x, z = lax.div(ep, NZ), lax.rem(ep, NZ)

    def up_x(d):
        return lax.rem(x + d + NX, NX)

    def up_y(d):
        return lax.rem(y + d + NY, NY)

    def up_z(d):
        return lax.rem(z + d + NZ, NZ)

    def dev(dx=0, dy=0, dz=0, dc=0):
        return (
            up_y(dy) * NC + lax.rem(c + dc, NC),
            up_x(dx) * NZ + up_z(dz),
        )

    sib = dev(dc=1)
    other = lax.rem(c + 1, NC)
    barrier = pltpu.get_barrier_semaphore()
    partners = [sib, dev(dx=1), dev(dx=-1), dev(dy=1), dev(dy=-1), dev(dz=1), dev(dz=-1)]
    for partner in partners:
        pl.semaphore_signal(barrier, inc=1, device_id=partner, device_id_type=MESH)
    meta_all[z, c, 0:8] = ids_in[...].astype(F32)
    meta_all[z, c, 8:16] = weights_in[...]
    pl.semaphore_wait(barrier, len(partners))
    net = Net(send_sems, recv_sems)

    blocks = (tok_all, grd_all)
    firsts = (tok, grd)
    ring, sibs = {}, {}

    def z_send(way, a, s):
        d = SIGNS[way]
        block = blocks[a].at[up_z(-d * s), c]
        src = firsts[a] if s == 0 else block
        ring[way, a, s] = net.put(src, block, dev(dz=d))
        if a == 0:
            note = meta_all.at[up_z(-d * s), c]
            ring[way, 2, s] = net.put(note, note, dev(dz=d))

    def z_step(a, s):
        for way in range(2):
            if s < LAST[way][a]:
                off = -SIGNS[way] * (s + 1)
                where = up_z(off)
                block = blocks[a].at[where, c]
                net.got(ring[way, a, s], block)
                if a == 0:
                    net.got(ring[way, 2, s], meta_all.at[where, c])
                if s + 1 < LAST[way][a]:
                    z_send(way, a, s + 1)
                share(a, off, block)

    def share(a, off, src):
        where = up_z(off)
        sibs[a, off % NZ] = net.put(src, blocks[a].at[where, c], sib)
        if a == 0:
            note = meta_all.at[where, c]
            sibs[2, off % NZ] = net.put(note, note, sib)

    for a in range(2):
        for way in range(2):
            z_send(way, a, 0)
    rings_x = {}

    def x_send(name, way, s, src, dst):
        rings_x[name, way, s] = net.put(src, dst, dev(dx=SIGNS[way]))

    quarter = ((uw, wu), (dw, wd))
    for h in range(2):
        for m in range(2):
            for way in range(2):
                x_send((m, h), way, 0, quarter[m][0].at[c, 2 * y + h], quarter[m][1].at[x, 2 * y + h])
    for h in range(2):
        for way in range(2):
            part = pl.ds(4 * h, 4)
            x_send((2, h), way, 0, gw.at[c, part], wg.at[x, part])
    for a in range(2):
        share(a, 0, firsts[a])
    local = [
        pltpu.make_async_copy(src, dst, local_sems.at[i])
        for i, (src, dst) in enumerate(
            (
                (tok, tok_all.at[z, c]),
                (grd, grd_all.at[z, c]),
                (gw.at[c], wg.at[x]),
                (uw.at[c], wu.at[x]),
                (dw.at[c], wd.at[x]),
            )
        )
    ]
    for copy in local:
        copy.start()

    rings_y = {}

    def y_send(name, way, s, ref):
        rings_y[name, way, s] = net.put(ref, ref, dev(dy=SIGNS[way]))

    def x_take_quarters(way):
        d = SIGNS[way]
        for h in range(2):
            for m in range(2):
                piece = quarter[m][1].at[up_x(-d), 2 * y + h]
                net.got(rings_x[(m, h), way, 0], piece)
                if h == way:
                    x_send((m, h), way, 1, piece, piece)
                for to in range(2):
                    y_send((m, h, -d), to, 0, piece)

    def x_take_far():
        for m in range(2):
            for way in range(2):
                piece = quarter[m][1].at[up_x(2), 2 * y + way]
                net.got(rings_x[(m, way), way, 1], piece)
                for to in range(2):
                    y_send((m, way, 2), to, 0, piece)

    def y_take(dx):
        for m in range(2):
            for way in range(2):
                for h in range(2):
                    piece = quarter[m][1].at[up_x(dx), 2 * up_y(-SIGNS[way]) + h]
                    net.got(rings_y[(m, h, dx), way, 0], piece)
                    if h == way:
                        y_send((m, h, dx), way, 1, piece)

    def y_take_far(dx):
        for m in range(2):
            for way in range(2):
                piece = quarter[m][1].at[up_x(dx), 2 * up_y(2) + way]
                net.got(rings_y[(m, way, dx), way, 1], piece)

    def x_take_gate():
        for way in range(2):
            for h in range(2):
                piece = wg.at[up_x(-SIGNS[way]), pl.ds(4 * h, 4)]
                net.got(rings_x[(2, h), way, 0], piece)
                if h == way:
                    x_send((2, h), way, 1, piece, piece)

    def x_take_gate_far():
        for way in range(2):
            piece = wg.at[up_x(2), pl.ds(4 * way, 4)]
            net.got(rings_x[(2, way), way, 1], piece)

    expert_col = lax.broadcasted_iota(jnp.int32, (8, PAIR), 0)
    names = jnp.where(expert_col < NX, 2 * (expert_col * NZ + z) + c, -1).astype(F32)
    t_row = lax.broadcasted_iota(jnp.int32, (PAIR, PAIR), 0)
    t_col = lax.broadcasted_iota(jnp.int32, (PAIR, PAIR), 1)
    same = (t_row < TOK) == (t_col < TOK)
    earlier = jnp.where((t_row < t_col) & same, 1.0, 0.0).astype(BF)
    base = jnp.where(lax.broadcasted_iota(jnp.int32, (8, PAIR), 1) < TOK, 0.0, float(CAP))
    slot_no = lax.broadcasted_iota(jnp.int32, (SLOTS, PAIR), 0).astype(F32)

    def ids_of(p):
        return jnp.concatenate([meta_all[p, 0, 0:8], meta_all[p, 1, 0:8]], axis=1)

    def pack(off):
        p = up_z(off)
        for a in range(2):
            net.got(sibs[a, off % NZ], blocks[a].at[p, other])
        net.got(sibs[2, off % NZ], meta_all.at[p, other])
        ids = ids_of(p)
        weights = jnp.concatenate([meta_all[p, 0, 8:16], meta_all[p, 1, 8:16]], axis=1)
        hot, w8 = jnp.zeros((8, PAIR), F32), jnp.zeros((8, PAIR), F32)
        for k in range(TOP):
            hit = ids[k : k + 1] == names
            hot = hot + jnp.where(hit, 1.0, 0.0)
            w8 = w8 + jnp.where(hit, weights[k : k + 1], 0.0)
        rank = nn(hot.astype(BF), earlier)
        slot = jnp.where(hot > 0.5, rank + base, -1.0)
        rows, scales = [], []
        for i in range(NX):
            one = jnp.where(slot[i : i + 1] == slot_no, 1.0, 0.0)
            rows.append(one)
            scales.append(jnp.sum(one * w8[i : i + 1], axis=1, keepdims=True))
        pt = jnp.concatenate(rows, axis=0).astype(BF)
        scale = jnp.concatenate(scales, axis=0)
        pts[p] = pt
        w8s[p] = w8
        at = pl.ds(pl.multiple_of(p * SLOTS, 16), SLOTS)
        packed = nn(pt, tok_all[p].reshape(PAIR, D)).astype(BF)
        xs[:, at, :] = packed.reshape(NX, SLOTS, D)
        scaled = (nn(pt, grd_all[p].reshape(PAIR, D)) * scale).astype(BF)
        ors[:, at, :] = scaled.reshape(NX, SLOTS, D)

    def expert(dx):
        i = up_x(dx)
        gate_w, up_w = wg[i].reshape(D, FF), wu[i].reshape(D, FF)
        down_w = wd[i].reshape(FF, D)
        rows, outs = xs[i], ors[i]
        gate_pre, up_pre = nn(rows, gate_w), nn(rows, up_w)
        sig = jax.nn.sigmoid(gate_pre)
        silu = gate_pre * sig
        slope = sig * (1.0 + gate_pre * (1.0 - sig))
        hidden = (silu * up_pre).astype(BF)
        hidden_grad = nt(outs, down_w)
        gate_delta = (hidden_grad * up_pre * slope).astype(BF)
        up_delta = (hidden_grad * silu).astype(BF)
        igs[i] = (nt(gate_delta, gate_w) + nt(up_delta, up_w)).astype(BF)
        expert_out = nn(hidden, down_w).astype(BF)
        wd[i] = expert_out.reshape(8, ROWS // 8, D)
        wg[i, 0:3] = hidden.reshape(3, TOK, FF)
        wu[i, 0:3] = gate_delta.reshape(3, TOK, FF)
        wu[i, 3:6] = up_delta.reshape(3, TOK, FF)

    def weight_grads(dx):
        i = up_x(dx)
        rows, outs = xs[i], ors[i]
        for m in range(2):
            delta = wu[i, 3 * m : 3 * m + 3].reshape(ROWS, FF)
            gx[i, :, :, m] = tn(rows, delta).astype(BF).reshape(NY, 2, TOK, FF)
        hidden = wg[i, 0:3].reshape(ROWS, FF)
        gd[i] = tn(hidden, outs).astype(BF).reshape(NY, 2, FF // 8, D)

    parts = (tok_all, grd_all)
    sib_bufs = (sib_l, sib_t)
    sib_tickets = {}

    def combine(off):
        p = up_z(off)
        ids = ids_of(p)
        pt, w8 = pts[p].astype(F32), w8s[p]
        outs = wd[:, p].reshape(NX * SLOTS, D)
        at = pl.ds(pl.multiple_of(p * SLOTS, 16), SLOTS)
        ins = igs[:, at, :].reshape(NX * SLOTS, D)
        weighted = jnp.concatenate(
            [pt[i * SLOTS : (i + 1) * SLOTS] * w8[i : i + 1] for i in range(NX)], axis=0
        ).astype(BF)
        dots = nt(outs, grd_all[p].reshape(PAIR, D)) * pt
        route = jnp.zeros((8, PAIR), F32)
        for i in range(NX):
            value = jnp.sum(dots[i * SLOTS : (i + 1) * SLOTS], axis=0, keepdims=True)
            route = route + jnp.where(ids == names[i : i + 1], value, 0.0)
        rp[p, 0] = route[:, :TOK]
        rp[p, 1] = route[:, TOK:]
        tok_all[p] = tn(weighted, outs).astype(BF).reshape(2, TOK, D)
        grd_all[p] = tn(pts[p], ins).astype(BF).reshape(2, TOK, D)
        for a in range(2):
            sib_tickets[a, off % NZ] = net.put(parts[a].at[p, other], sib_bufs[a].at[p], sib)
        sib_tickets[2, off % NZ] = net.put(rp.at[p, other], sib_r.at[p], sib)

    z_step(0, 0)
    x_take_quarters(0)
    x_take_quarters(1)
    for copy in local:
        copy.wait()
    z_step(1, 0)
    x_take_far()
    pack(0)
    z_step(0, 1)
    y_take(-1)
    pack(1)
    pack(-1)
    z_step(1, 1)
    y_take(1)
    z_step(0, 2)
    x_take_gate()
    y_take(2)
    pack(2)
    pack(-2)
    z_step(1, 2)
    y_take_far(-1)
    y_take_far(1)
    z_step(0, 3)
    pack(3)
    pack(-3)
    z_step(1, 3)
    y_take_far(2)
    x_take_gate_far()
    pack(4)
    net.drain()

    grads = (gx, gd)
    chain, tickets = {}, {}
    buf_no = {}
    for way in range(2):
        for a in range(2):
            for s in range(LAST[way][a]):
                buf_no[way, a, s] = len(buf_no)

    def add(ref, *more):
        total = ref[...].astype(F32)
        for m in more:
            total = total + m[...].astype(F32)
        ref[...] = total.astype(BF)

    def z_pass(way, a, s):
        d = SIGNS[way]
        off = d * (LAST[way][a] - s)
        where = up_z(off)
        net.got(sib_tickets[a, off % NZ], sib_bufs[a].at[where])
        block = parts[a].at[where, c]
        more = [sib_bufs[a].at[where]]
        if s > 0:
            came = rz.at[buf_no[way, a, s - 1]]
            net.got(chain[way, a, s - 1], came)
            more.append(came)
        add(block, *more)
        chain[way, a, s] = net.put(block, rz.at[buf_no[way, a, s]], dev(dz=d))
        if a == 0:
            net.got(sib_tickets[2, off % NZ], sib_r.at[where])
            route = rp[where, c] + sib_r[where]
            if s > 0:
                net.got(chain[way, 2, s - 1], zr.at[buf_no[way, 0, s - 1]])
                route = route + zr[buf_no[way, 0, s - 1]]
            rp[where, c] = route
            chain[way, 2, s] = net.put(
                rp.at[where, c], zr.at[buf_no[way, 0, s]], dev(dz=d)
            )

    half = (pl.ds(0, 2), pl.ds(2, 2))
    far_x, near_x = (xfx, xfd), (xnx, xnd)
    far_y, near_y = (yfx, yfd), (ynx, ynd)
    second = (sx, sd)

    def y_way(dx):
        return 0 if dx in (2, 1) else 1

    def grad_send(dx):
        i = up_x(dx)
        for g in range(2):
            if dx == 2:
                for way in range(2):
                    tickets["xf", way, g] = net.put(
                        grads[g].at[i, half[way], 0], far_x[g].at[way], dev(dx=SIGNS[way])
                    )
            elif dx:
                way = SIGNS.index(dx)
                free = half[1 - way]
                tickets["xa", way, g] = net.put(
                    grads[g].at[i, free, 0], near_x[g].at[way, free], dev(dx=dx)
                )
            way = y_way(dx)
            tickets["yf", dx, g] = net.put(
                grads[g].at[i, up_y(2), 1], far_y[g].at[dx % NX], dev(dy=SIGNS[way])
            )
            tickets["yn", dx, 1 - way, g] = net.put(
                grads[g].at[i, up_y(SIGNS[1 - way]), 1],
                near_y[g].at[dx % NX, 1 - way],
                dev(dy=SIGNS[1 - way]),
            )

    def x_pass(way):
        i = up_x(SIGNS[way])
        for g in range(2):
            net.got(tickets["xf", way, g], far_x[g].at[way])
            mine = grads[g].at[i, half[way], 0]
            add(mine, far_x[g].at[way])
            tickets["xb", way, g] = net.put(
                mine, near_x[g].at[way, half[way]], dev(dx=SIGNS[way])
            )

    def y_pass(dx):
        way = y_way(dx)
        for g in range(2):
            net.got(tickets["yf", dx, g], far_y[g].at[dx % NX])
            mine = grads[g].at[up_x(dx), up_y(SIGNS[way]), 1]
            add(mine, far_y[g].at[dx % NX])
            tickets["yn", dx, way, g] = net.put(
                mine, near_y[g].at[dx % NX, way], dev(dy=SIGNS[way])
            )

    def second_view(h, g, d):
        return grads[g].at[x, up_y(d), 0] if h == 0 else grads[g].at[up_x(d), y, 1]

    def second_dev(h, way):
        return dev(dy=SIGNS[way]) if h == 0 else dev(dx=SIGNS[way])

    def second_send(h, g):
        way = g
        tickets["sf", h, g] = net.put(
            second_view(h, g, 2), second[g].at[h, 2], second_dev(h, way)
        )
        tickets["sn", h, g, 1 - way] = net.put(
            second_view(h, g, SIGNS[1 - way]), second[g].at[h, 1 - way], second_dev(h, 1 - way)
        )

    def x_last():
        for g in range(2):
            for way in range(2):
                net.got(tickets["xa", way, g], near_x[g].at[way, half[1 - way]])
                net.got(tickets["xb", way, g], near_x[g].at[way, half[way]])
            add(grads[g].at[x, :, 0], near_x[g].at[0], near_x[g].at[1])
            second_send(0, g)

    def y_last():
        for g in range(2):
            for dx in (2, 1, -1, 0):
                for way in range(2):
                    net.got(tickets["yn", dx, way, g], near_y[g].at[dx % NX, way])
                near = near_y[g].at[dx % NX]
                add(grads[g].at[up_x(dx), y, 1], near.at[0], near.at[1])
            second_send(1, g)

    def second_pass(h):
        for g in range(2):
            way = g
            net.got(tickets["sf", h, g], second[g].at[h, 2])
            mine = second_view(h, g, SIGNS[way])
            add(mine, second[g].at[h, 2])
            tickets["sn", h, g, way] = net.put(
                mine, second[g].at[h, way], second_dev(h, way)
            )

    expert(2)
    weight_grads(2)
    grad_send(2)
    expert(1)
    expert(-1)
    expert(0)
    combine(4)
    combine(3)
    combine(-3)
    z_pass(0, 0, 0)
    z_pass(1, 1, 0)
    z_pass(0, 1, 0)
    z_pass(1, 0, 0)
    weight_grads(1)
    grad_send(1)
    weight_grads(-1)
    grad_send(-1)
    x_pass(0)
    x_pass(1)
    combine(2)
    combine(-2)
    z_pass(0, 0, 1)
    z_pass(1, 1, 1)
    weight_grads(0)
    grad_send(0)
    z_pass(0, 1, 1)
    z_pass(1, 0, 1)
    y_pass(2)
    y_pass(1)
    y_pass(-1)
    combine(1)
    combine(-1)
    z_pass(0, 0, 2)
    z_pass(1, 1, 2)
    y_pass(0)
    x_last()
    z_pass(0, 1, 2)
    z_pass(1, 0, 2)
    combine(0)
    y_last()
    z_pass(0, 0, 3)
    z_pass(1, 1, 3)
    second_pass(0)
    second_pass(1)

    results = (lo, tg)
    for a in range(2):
        net.got(sib_tickets[a, 0], sib_bufs[a].at[z])
        total = parts[a][z, c].astype(F32) + sib_bufs[a][z].astype(F32)
        for way in range(2):
            s = LAST[way][a] - 1
            came = rz.at[buf_no[way, a, s]]
            net.got(chain[way, a, s], came)
            total = total + came[...].astype(F32)
        results[a][...] = total.astype(BF)
    net.got(sib_tickets[2, 0], sib_r.at[z])
    total = rp[z, c] + sib_r[z]
    for way in range(2):
        no = buf_no[way, 0, LAST[way][0] - 1]
        net.got(chain[way, 2, LAST[way][0] - 1], zr.at[no])
        total = total + zr[no]
    rg[...] = total

    finals = ((go, uo), (do,))
    stage = (hx, hd)
    hand = []
    for g in range(2):
        both = []
        for h in range(2):
            for way in range(2):
                net.got(tickets["sn", h, g, way], second[g].at[h, way])
            both.append(
                second_view(h, g, 0)[...].astype(F32)
                + second[g][h, 0].astype(F32)
                + second[g][h, 1].astype(F32)
            )
        keep = jnp.where(c == 0, both[0], both[1])
        away = jnp.where(c == 0, both[1], both[0])
        stage[g][0] = away.astype(BF)
        hand.append(net.put(stage[g].at[0], stage[g].at[1], sib))
        if g == 0:
            go[c], uo[c] = keep[0], keep[1]
        else:
            do[c] = keep
    net.got(hand[0], hx.at[1])
    go[other] = hx[1, 0].astype(F32)
    uo[other] = hx[1, 1].astype(F32)
    net.got(hand[1], hd.at[1])
    do[other] = hd[1].astype(F32)
    net.drain()


def hand_out(*refs):
    n = len(refs) // 2
    for i in range(n):
        refs[n + i][...] = refs[i][...]


def per_device(tokens, expert_ids, route_weights, out_grad, gate_weight, up_weight, down_weight):
    gate_weight = gate_weight.reshape(2, 8, D // 8, FF)
    up_weight = up_weight.reshape(2, 8, D // 8, FF)
    down_weight = down_weight.reshape(2, 8, FF // 8, D)
    vmem = pl.BlockSpec(memory_space=pltpu.VMEM)
    hbm = pl.BlockSpec(memory_space=pl.ANY)
    wide, tall = (D // 8, FF), (FF // 8, D)
    two = (2, *wide)
    out_shape = (
        jax.ShapeDtypeStruct((TOK, D), BF),
        jax.ShapeDtypeStruct((TOK, D), BF),
        jax.ShapeDtypeStruct((TOP, TOK), F32),
        jax.ShapeDtypeStruct((2, *wide), F32),
        jax.ShapeDtypeStruct((2, *wide), F32),
        jax.ShapeDtypeStruct((2, *tall), F32),
    )
    results = pl.pallas_call(
        kernel,
        out_shape=out_shape,
        in_specs=[vmem, vmem, vmem, vmem, hbm, hbm, hbm],
        out_specs=(vmem,) * 6,
        scratch_shapes=[
            pltpu.VMEM((NZ, NC, TOK, D), BF),
            pltpu.VMEM((NZ, NC, TOK, D), BF),
            pltpu.VMEM((NZ, NC, 16, TOK), F32),
            pltpu.VMEM((NX, 8, *wide), BF),
            pltpu.VMEM((NX, 8, *wide), BF),
            pltpu.VMEM((NX, 8, *tall), BF),
            pltpu.VMEM((NX, ROWS, D), BF),
            pltpu.VMEM((NX, ROWS, D), BF),
            pltpu.VMEM((NX, ROWS, D), BF),
            pltpu.VMEM((NZ, NX * SLOTS, PAIR), BF),
            pltpu.VMEM((NZ, 8, PAIR), F32),
            pltpu.VMEM((NX, NY, 2, *two), BF),
            pltpu.VMEM((NX, NY, 2, *tall), BF),
            pltpu.VMEM((NZ, TOK, D), BF),
            pltpu.VMEM((NZ, TOK, D), BF),
            pltpu.VMEM((NZ, TOP, TOK), F32),
            pltpu.VMEM((14, TOK, D), BF),
            pltpu.VMEM((14, TOP, TOK), F32),
            pltpu.VMEM((NZ, NC, TOP, TOK), F32),
            *[pltpu.VMEM((2, 2, *s), BF) for s in (two, tall)],
            *[pltpu.VMEM((2, 4, *s), BF) for s in (two, tall)],
            *[pltpu.VMEM((4, *s), BF) for s in (two, tall)],
            *[pltpu.VMEM((4, 2, *s), BF) for s in (two, tall)],
            *[pltpu.VMEM((2, 3, *s), BF) for s in (two, tall)],
            *[pltpu.VMEM((2, *s), BF) for s in (two, tall)],
            pltpu.SemaphoreType.DMA((N_SEND,)),
            pltpu.SemaphoreType.DMA((N_RECV,)),
            pltpu.SemaphoreType.DMA((5,)),
        ],
        compiler_params=pltpu.CompilerParams(
            collective_id=0,
            has_side_effects=True,
            vmem_limit_bytes=63 * 1024 * 1024,
        ),
    )(tokens, out_grad, expert_ids.T, route_weights.T, gate_weight, up_weight, down_weight)
    layer_out, token_grad, route_grad, gate_share, up_share, down_share = pl.pallas_call(
        hand_out,
        out_shape=out_shape,
        in_specs=[vmem] * 6,
        out_specs=(vmem,) * 6,
    )(*results)
    return (layer_out, token_grad, route_grad.T, gate_share, up_share, down_share)


def solution(mesh):
    return jax.shard_map(
        per_device,
        mesh=mesh,
        in_specs=(
            P(("rep", "ep"), None),
            P(("rep", "ep"), None),
            P(("rep", "ep"), None),
            P(("rep", "ep"), None),
            P("ep", None, None),
            P("ep", None, None),
            P("ep", None, None),
        ),
        out_specs=(
            P(("rep", "ep"), None),
            P(("rep", "ep"), None),
            P(("rep", "ep"), None),
            P("ep", "rep", None),
            P("ep", "rep", None),
            P("ep", "rep", None),
        ),
        check_vma=False,
    )
```

```python
import jax
import jax.numpy as jnp
from jax import lax
from jax.experimental import pallas as pl
from jax.experimental.pallas import tpu as pltpu
from jax.sharding import PartitionSpec as P

MESH = pl.DeviceIdType.MESH
NX, NY, NZ, NC = 4, 4, 8, 2
TOK, D, FF, TOP, CAP = 128, 1024, 384, 8, 24
PAIR = 2 * TOK
SLOTS = 2 * CAP
ROWS = NZ * SLOTS
BF = jnp.bfloat16
F32 = jnp.float32


def nn(a, b):
    return lax.dot_general(a, b, (((1,), (0,)), ((), ())), preferred_element_type=F32)


def nt(a, b):
    return lax.dot_general(a, b, (((1,), (1,)), ((), ())), preferred_element_type=F32)


def tn(a, b):
    return lax.dot_general(a, b, (((0,), (0,)), ((), ())), preferred_element_type=F32)


class Net:
    def __init__(self, send, recv):
        self.send_sems, self.recv_sems = send, recv
        self.sent = self.count = 0
        self.pending = []

    def copy(self, src, dst, dev, out, into):
        return pltpu.make_async_remote_copy(
            src_ref=src,
            dst_ref=dst,
            send_sem=self.send_sems.at[out],
            recv_sem=self.recv_sems.at[into],
            device_id=dev,
            device_id_type=MESH,
        )

    def put(self, src, dst, dev):
        copy = self.copy(src, dst, dev, self.sent, self.count)
        copy.start()
        self.pending.append(copy)
        self.sent, self.count = self.sent + 1, self.count + 1
        return self.count - 1, dev

    def got(self, ticket, dst):
        into, dev = ticket
        self.copy(dst, dst, dev, 0, into).wait_recv()

    def drain(self):
        for copy in self.pending:
            copy.wait_send()
        self.pending, self.sent = [], 0


N_SEND, N_RECV = 99, 194
SIGNS = (1, -1)
LAST = ((4, 3), (3, 4))


def kernel(
    tok, grd, ids_in, weights_in, gw, uw, dw,
    lo, tg, rg, go, uo, do,
    tok_all, grd_all, meta_all, wg, wu, wd, xs, ors, igs, pts, w8s,
    gx, gd, sib_l, sib_t, sib_r, rz, zr, rp,
    xfx, xfd, xnx, xnd, yfx, yfd, ynx, ynd, sx, sd, hx, hd,
    send_sems, recv_sems, local_sems,
):
    rep, ep = lax.axis_index("rep"), lax.axis_index("ep")
    y, c = lax.div(rep, NC), lax.rem(rep, NC)
    x, z = lax.div(ep, NZ), lax.rem(ep, NZ)

    def up_x(d):
        return lax.rem(x + d + NX, NX)

    def up_y(d):
        return lax.rem(y + d + NY, NY)

    def up_z(d):
        return lax.rem(z + d + NZ, NZ)

    def dev(dx=0, dy=0, dz=0, dc=0):
        return (
            up_y(dy) * NC + lax.rem(c + dc, NC),
            up_x(dx) * NZ + up_z(dz),
        )

    sib = dev(dc=1)
    other = lax.rem(c + 1, NC)
    barrier = pltpu.get_barrier_semaphore()
    partners = [sib, dev(dx=1), dev(dx=-1), dev(dy=1), dev(dy=-1), dev(dz=1), dev(dz=-1)]
    for partner in partners:
        pl.semaphore_signal(barrier, inc=1, device_id=partner, device_id_type=MESH)
    meta_all[z, c, 0:8] = ids_in[...].astype(F32)
    meta_all[z, c, 8:16] = weights_in[...]
    pl.semaphore_wait(barrier, len(partners))
    net = Net(send_sems, recv_sems)

    blocks = (tok_all, grd_all)
    firsts = (tok, grd)
    ring, sibs = {}, {}

    def z_send(way, a, s):
        d = SIGNS[way]
        block = blocks[a].at[up_z(-d * s), c]
        src = firsts[a] if s == 0 else block
        ring[way, a, s] = net.put(src, block, dev(dz=d))
        if a == 0:
            note = meta_all.at[up_z(-d * s), c]
            ring[way, 2, s] = net.put(note, note, dev(dz=d))

    def z_step(a, s):
        for way in range(2):
            if s < LAST[way][a]:
                off = -SIGNS[way] * (s + 1)
                where = up_z(off)
                block = blocks[a].at[where, c]
                net.got(ring[way, a, s], block)
                if a == 0:
                    net.got(ring[way, 2, s], meta_all.at[where, c])
                if s + 1 < LAST[way][a]:
                    z_send(way, a, s + 1)
                share(a, off, block)

    def share(a, off, src):
        where = up_z(off)
        sibs[a, off % NZ] = net.put(src, blocks[a].at[where, c], sib)
        if a == 0:
            note = meta_all.at[where, c]
            sibs[2, off % NZ] = net.put(note, note, sib)

    for a in range(2):
        for way in range(2):
            z_send(way, a, 0)
    rings_x = {}

    def x_send(name, way, s, src, dst):
        rings_x[name, way, s] = net.put(src, dst, dev(dx=SIGNS[way]))

    quarter = ((uw, wu), (dw, wd))
    for h in range(2):
        for m in range(2):
            for way in range(2):
                x_send((m, h), way, 0, quarter[m][0].at[c, 2 * y + h], quarter[m][1].at[x, 2 * y + h])
    for a in range(2):
        share(a, 0, firsts[a])
    local = [
        pltpu.make_async_copy(src, dst, local_sems.at[i])
        for i, (src, dst) in enumerate(
            (
                (tok, tok_all.at[z, c]),
                (grd, grd_all.at[z, c]),
                (gw.at[c], wg.at[x]),
                (uw.at[c], wu.at[x]),
                (dw.at[c], wd.at[x]),
            )
        )
    ]
    for copy in local:
        copy.start()

    rings_y = {}

    def y_send(name, way, s, ref):
        rings_y[name, way, s] = net.put(ref, ref, dev(dy=SIGNS[way]))

    def x_take_quarters(way):
        d = SIGNS[way]
        for h in range(2):
            for m in range(2):
                piece = quarter[m][1].at[up_x(-d), 2 * y + h]
                net.got(rings_x[(m, h), way, 0], piece)
                if h == way:
                    x_send((m, h), way, 1, piece, piece)
                for to in range(2):
                    y_send((m, h, -d), to, 0, piece)

    def x_take_far():
        for m in range(2):
            for way in range(2):
                piece = quarter[m][1].at[up_x(2), 2 * y + way]
                net.got(rings_x[(m, way), way, 1], piece)
                for to in range(2):
                    y_send((m, way, 2), to, 0, piece)

    def y_take(dx):
        for m in range(2):
            for way in range(2):
                for h in range(2):
                    piece = quarter[m][1].at[up_x(dx), 2 * up_y(-SIGNS[way]) + h]
                    net.got(rings_y[(m, h, dx), way, 0], piece)
                    if h == way:
                        y_send((m, h, dx), way, 1, piece)

    def y_take_far(dx):
        for m in range(2):
            for way in range(2):
                piece = quarter[m][1].at[up_x(dx), 2 * up_y(2) + way]
                net.got(rings_y[(m, way, dx), way, 1], piece)

    def x_take_gate():
        for way in range(2):
            for h in range(2):
                piece = wg.at[up_x(-SIGNS[way]), pl.ds(4 * h, 4)]
                net.got(rings_x[(2, h), way, 0], piece)
                if h == way:
                    x_send((2, h), way, 1, piece, piece)

    def x_take_gate_far():
        for way in range(2):
            piece = wg.at[up_x(2), pl.ds(4 * way, 4)]
            net.got(rings_x[(2, way), way, 1], piece)

    expert_col = lax.broadcasted_iota(jnp.int32, (8, PAIR), 0)
    names = jnp.where(expert_col < NX, 2 * (expert_col * NZ + z) + c, -1).astype(F32)
    t_row = lax.broadcasted_iota(jnp.int32, (PAIR, PAIR), 0)
    t_col = lax.broadcasted_iota(jnp.int32, (PAIR, PAIR), 1)
    same = (t_row < TOK) == (t_col < TOK)
    earlier = jnp.where((t_row < t_col) & same, 1.0, 0.0).astype(BF)
    base = jnp.where(lax.broadcasted_iota(jnp.int32, (8, PAIR), 1) < TOK, 0.0, float(CAP))
    slot_no = lax.broadcasted_iota(jnp.int32, (SLOTS, PAIR), 0).astype(F32)

    def ids_of(p):
        return jnp.concatenate([meta_all[p, 0, 0:8], meta_all[p, 1, 0:8]], axis=1)

    def pack(off):
        p = up_z(off)
        for a in range(2):
            net.got(sibs[a, off % NZ], blocks[a].at[p, other])
        net.got(sibs[2, off % NZ], meta_all.at[p, other])
        ids = ids_of(p)
        weights = jnp.concatenate([meta_all[p, 0, 8:16], meta_all[p, 1, 8:16]], axis=1)
        hot, w8 = jnp.zeros((8, PAIR), F32), jnp.zeros((8, PAIR), F32)
        for k in range(TOP):
            hit = ids[k : k + 1] == names
            hot = hot + jnp.where(hit, 1.0, 0.0)
            w8 = w8 + jnp.where(hit, weights[k : k + 1], 0.0)
        rank = nn(hot.astype(BF), earlier)
        slot = jnp.where(hot > 0.5, rank + base, -1.0)
        rows, scales = [], []
        for i in range(NX):
            one = jnp.where(slot[i : i + 1] == slot_no, 1.0, 0.0)
            rows.append(one)
            scales.append(jnp.sum(one * w8[i : i + 1], axis=1, keepdims=True))
        pt = jnp.concatenate(rows, axis=0).astype(BF)
        scale = jnp.concatenate(scales, axis=0)
        pts[p] = pt
        w8s[p] = w8
        at = pl.ds(pl.multiple_of(p * SLOTS, 16), SLOTS)
        packed = nn(pt, tok_all[p].reshape(PAIR, D)).astype(BF)
        xs[:, at, :] = packed.reshape(NX, SLOTS, D)
        scaled = (nn(pt, grd_all[p].reshape(PAIR, D)) * scale).astype(BF)
        ors[:, at, :] = scaled.reshape(NX, SLOTS, D)

    def expert(dx):
        i = up_x(dx)
        gate_w, up_w = wg[i].reshape(D, FF), wu[i].reshape(D, FF)
        down_w = wd[i].reshape(FF, D)
        rows, outs = xs[i], ors[i]
        gate_pre, up_pre = nn(rows, gate_w), nn(rows, up_w)
        sig = jax.nn.sigmoid(gate_pre)
        silu = gate_pre * sig
        slope = sig * (1.0 + gate_pre * (1.0 - sig))
        hidden = (silu * up_pre).astype(BF)
        hidden_grad = nt(outs, down_w)
        gate_delta = (hidden_grad * up_pre * slope).astype(BF)
        up_delta = (hidden_grad * silu).astype(BF)
        igs[i] = (nt(gate_delta, gate_w) + nt(up_delta, up_w)).astype(BF)
        expert_out = nn(hidden, down_w).astype(BF)
        wd[i] = expert_out.reshape(8, ROWS // 8, D)
        wg[i, 0:3] = hidden.reshape(3, TOK, FF)
        wu[i, 0:3] = gate_delta.reshape(3, TOK, FF)
        wu[i, 3:6] = up_delta.reshape(3, TOK, FF)

    def weight_grads(dx):
        i = up_x(dx)
        rows, outs = xs[i], ors[i]
        for m in range(2):
            delta = wu[i, 3 * m : 3 * m + 3].reshape(ROWS, FF)
            gx[i, :, :, m] = tn(rows, delta).astype(BF).reshape(NY, 2, TOK, FF)
        hidden = wg[i, 0:3].reshape(ROWS, FF)
        gd[i] = tn(hidden, outs).astype(BF).reshape(NY, 2, FF // 8, D)

    parts = (tok_all, grd_all)
    sib_bufs = (sib_l, sib_t)
    sib_tickets = {}

    def combine(off):
        p = up_z(off)
        ids = ids_of(p)
        pt, w8 = pts[p].astype(F32), w8s[p]
        outs = wd[:, p].reshape(NX * SLOTS, D)
        at = pl.ds(pl.multiple_of(p * SLOTS, 16), SLOTS)
        ins = igs[:, at, :].reshape(NX * SLOTS, D)
        weighted = jnp.concatenate(
            [pt[i * SLOTS : (i + 1) * SLOTS] * w8[i : i + 1] for i in range(NX)], axis=0
        ).astype(BF)
        dots = nt(outs, grd_all[p].reshape(PAIR, D)) * pt
        route = jnp.zeros((8, PAIR), F32)
        for i in range(NX):
            value = jnp.sum(dots[i * SLOTS : (i + 1) * SLOTS], axis=0, keepdims=True)
            route = route + jnp.where(ids == names[i : i + 1], value, 0.0)
        rp[p, 0] = route[:, :TOK]
        rp[p, 1] = route[:, TOK:]
        tok_all[p] = tn(weighted, outs).astype(BF).reshape(2, TOK, D)
        grd_all[p] = tn(pts[p], ins).astype(BF).reshape(2, TOK, D)
        for a in range(2):
            sib_tickets[a, off % NZ] = net.put(parts[a].at[p, other], sib_bufs[a].at[p], sib)
        sib_tickets[2, off % NZ] = net.put(rp.at[p, other], sib_r.at[p], sib)

    x_take_quarters(0)
    x_take_quarters(1)
    for h in range(2):
        for way in range(2):
            part = pl.ds(4 * h, 4)
            x_send((2, h), way, 0, gw.at[c, part], wg.at[x, part])
    z_step(0, 0)
    for copy in local:
        copy.wait()
    z_step(1, 0)
    x_take_far()
    pack(0)
    z_step(0, 1)
    y_take(-1)
    pack(1)
    pack(-1)
    z_step(1, 1)
    y_take(1)
    z_step(0, 2)
    x_take_gate()
    y_take(2)
    pack(2)
    pack(-2)
    z_step(1, 2)
    y_take_far(-1)
    y_take_far(1)
    z_step(0, 3)
    pack(3)
    pack(-3)
    z_step(1, 3)
    y_take_far(2)
    x_take_gate_far()
    pack(4)
    net.drain()

    grads = (gx, gd)
    chain, tickets = {}, {}
    buf_no = {}
    for way in range(2):
        for a in range(2):
            for s in range(LAST[way][a]):
                buf_no[way, a, s] = len(buf_no)

    def add(ref, *more):
        total = ref[...].astype(F32)
        for m in more:
            total = total + m[...].astype(F32)
        ref[...] = total.astype(BF)

    def z_pass(way, a, s):
        d = SIGNS[way]
        off = d * (LAST[way][a] - s)
        where = up_z(off)
        net.got(sib_tickets[a, off % NZ], sib_bufs[a].at[where])
        block = parts[a].at[where, c]
        more = [sib_bufs[a].at[where]]
        if s > 0:
            came = rz.at[buf_no[way, a, s - 1]]
            net.got(chain[way, a, s - 1], came)
            more.append(came)
        add(block, *more)
        chain[way, a, s] = net.put(block, rz.at[buf_no[way, a, s]], dev(dz=d))
        if a == 0:
            net.got(sib_tickets[2, off % NZ], sib_r.at[where])
            route = rp[where, c] + sib_r[where]
            if s > 0:
                net.got(chain[way, 2, s - 1], zr.at[buf_no[way, 0, s - 1]])
                route = route + zr[buf_no[way, 0, s - 1]]
            rp[where, c] = route
            chain[way, 2, s] = net.put(
                rp.at[where, c], zr.at[buf_no[way, 0, s]], dev(dz=d)
            )

    half = (pl.ds(0, 2), pl.ds(2, 2))
    far_x, near_x = (xfx, xfd), (xnx, xnd)
    far_y, near_y = (yfx, yfd), (ynx, ynd)
    second = (sx, sd)

    def y_way(dx):
        return 0 if dx in (2, -1) else 1

    def grad_send(dx):
        i = up_x(dx)
        for g in range(2):
            if dx == 2:
                for way in range(2):
                    tickets["xf", way, g] = net.put(
                        grads[g].at[i, half[way], 0], far_x[g].at[way], dev(dx=SIGNS[way])
                    )
            way = y_way(dx)
            tickets["yf", dx, g] = net.put(
                grads[g].at[i, up_y(2), 1], far_y[g].at[dx % NX], dev(dy=SIGNS[way])
            )
            tickets["yn", dx, 1 - way, g] = net.put(
                grads[g].at[i, up_y(SIGNS[1 - way]), 1],
                near_y[g].at[dx % NX, 1 - way],
                dev(dy=SIGNS[1 - way]),
            )

    def x_pass(way):
        i = up_x(SIGNS[way])
        for g in range(2):
            net.got(tickets["xf", way, g], far_x[g].at[way])
            mine = grads[g].at[i, half[way], 0]
            add(mine, far_x[g].at[way])
            tickets["xb", way, g] = net.put(
                mine, near_x[g].at[way, half[way]], dev(dx=SIGNS[way])
            )
            free = half[1 - way]
            tickets["xa", way, g] = net.put(
                grads[g].at[i, free, 0], near_x[g].at[way, free], dev(dx=SIGNS[way])
            )

    def y_pass(dx):
        way = y_way(dx)
        for g in range(2):
            net.got(tickets["yf", dx, g], far_y[g].at[dx % NX])
            mine = grads[g].at[up_x(dx), up_y(SIGNS[way]), 1]
            add(mine, far_y[g].at[dx % NX])
            tickets["yn", dx, way, g] = net.put(
                mine, near_y[g].at[dx % NX, way], dev(dy=SIGNS[way])
            )

    def second_view(h, g, d):
        return grads[g].at[x, up_y(d), 0] if h == 0 else grads[g].at[up_x(d), y, 1]

    def second_dev(h, way):
        return dev(dy=SIGNS[way]) if h == 0 else dev(dx=SIGNS[way])

    def second_send(h, g):
        way = g
        tickets["sf", h, g] = net.put(
            second_view(h, g, 2), second[g].at[h, 2], second_dev(h, way)
        )
        tickets["sn", h, g, 1 - way] = net.put(
            second_view(h, g, SIGNS[1 - way]), second[g].at[h, 1 - way], second_dev(h, 1 - way)
        )

    def x_last():
        for g in range(2):
            for way in range(2):
                net.got(tickets["xa", way, g], near_x[g].at[way, half[1 - way]])
                net.got(tickets["xb", way, g], near_x[g].at[way, half[way]])
            add(grads[g].at[x, :, 0], near_x[g].at[0], near_x[g].at[1])
            second_send(0, g)

    def y_last():
        for g in range(2):
            for dx in (2, 1, -1, 0):
                for way in range(2):
                    net.got(tickets["yn", dx, way, g], near_y[g].at[dx % NX, way])
                near = near_y[g].at[dx % NX]
                add(grads[g].at[up_x(dx), y, 1], near.at[0], near.at[1])
            second_send(1, g)

    def second_pass(h):
        for g in range(2):
            way = g
            net.got(tickets["sf", h, g], second[g].at[h, 2])
            mine = second_view(h, g, SIGNS[way])
            add(mine, second[g].at[h, 2])
            tickets["sn", h, g, way] = net.put(
                mine, second[g].at[h, way], second_dev(h, way)
            )

    expert(2)
    weight_grads(2)
    grad_send(2)
    expert(1)
    weight_grads(1)
    grad_send(1)
    expert(-1)
    expert(0)
    combine(4)
    combine(3)
    combine(-3)
    y_pass(2)
    z_pass(0, 0, 0)
    z_pass(1, 1, 0)
    z_pass(0, 1, 0)
    z_pass(1, 0, 0)
    x_pass(0)
    weight_grads(-1)
    grad_send(-1)
    x_pass(1)
    y_pass(1)
    weight_grads(0)
    grad_send(0)
    combine(2)
    combine(-2)
    z_pass(0, 0, 1)
    z_pass(1, 1, 1)
    z_pass(0, 1, 1)
    z_pass(1, 0, 1)
    y_pass(-1)
    combine(1)
    combine(-1)
    y_pass(0)
    z_pass(0, 0, 2)
    z_pass(1, 1, 2)
    z_pass(0, 1, 2)
    z_pass(1, 0, 2)
    combine(0)
    x_last()
    y_last()
    z_pass(0, 0, 3)
    z_pass(1, 1, 3)
    second_pass(0)
    second_pass(1)

    results = (lo, tg)
    for a in range(2):
        net.got(sib_tickets[a, 0], sib_bufs[a].at[z])
        total = parts[a][z, c].astype(F32) + sib_bufs[a][z].astype(F32)
        for way in range(2):
            s = LAST[way][a] - 1
            came = rz.at[buf_no[way, a, s]]
            net.got(chain[way, a, s], came)
            total = total + came[...].astype(F32)
        results[a][...] = total.astype(BF)
    net.got(sib_tickets[2, 0], sib_r.at[z])
    total = rp[z, c] + sib_r[z]
    for way in range(2):
        no = buf_no[way, 0, LAST[way][0] - 1]
        net.got(chain[way, 2, LAST[way][0] - 1], zr.at[no])
        total = total + zr[no]
    rg[...] = total

    finals = ((go, uo), (do,))
    stage = (hx, hd)
    hand = []
    for g in range(2):
        both = []
        for h in range(2):
            for way in range(2):
                net.got(tickets["sn", h, g, way], second[g].at[h, way])
            both.append(
                second_view(h, g, 0)[...].astype(F32)
                + second[g][h, 0].astype(F32)
                + second[g][h, 1].astype(F32)
            )
        keep = jnp.where(c == 0, both[0], both[1])
        away = jnp.where(c == 0, both[1], both[0])
        stage[g][0] = away.astype(BF)
        hand.append(net.put(stage[g].at[0], stage[g].at[1], sib))
        if g == 0:
            go[c], uo[c] = keep[0], keep[1]
        else:
            do[c] = keep
    net.got(hand[0], hx.at[1])
    go[other] = hx[1, 0].astype(F32)
    uo[other] = hx[1, 1].astype(F32)
    net.got(hand[1], hd.at[1])
    do[other] = hd[1].astype(F32)
    net.drain()


def hand_out(*refs):
    n = len(refs) // 2
    for i in range(n):
        refs[n + i][...] = refs[i][...]


def per_device(tokens, expert_ids, route_weights, out_grad, gate_weight, up_weight, down_weight):
    gate_weight = gate_weight.reshape(2, 8, D // 8, FF)
    up_weight = up_weight.reshape(2, 8, D // 8, FF)
    down_weight = down_weight.reshape(2, 8, FF // 8, D)
    vmem = pl.BlockSpec(memory_space=pltpu.VMEM)
    hbm = pl.BlockSpec(memory_space=pl.ANY)
    wide, tall = (D // 8, FF), (FF // 8, D)
    two = (2, *wide)
    out_shape = (
        jax.ShapeDtypeStruct((TOK, D), BF),
        jax.ShapeDtypeStruct((TOK, D), BF),
        jax.ShapeDtypeStruct((TOP, TOK), F32),
        jax.ShapeDtypeStruct((2, *wide), F32),
        jax.ShapeDtypeStruct((2, *wide), F32),
        jax.ShapeDtypeStruct((2, *tall), F32),
    )
    results = pl.pallas_call(
        kernel,
        out_shape=out_shape,
        in_specs=[vmem, vmem, vmem, vmem, hbm, hbm, hbm],
        out_specs=(vmem,) * 6,
        scratch_shapes=[
            pltpu.VMEM((NZ, NC, TOK, D), BF),
            pltpu.VMEM((NZ, NC, TOK, D), BF),
            pltpu.VMEM((NZ, NC, 16, TOK), F32),
            pltpu.VMEM((NX, 8, *wide), BF),
            pltpu.VMEM((NX, 8, *wide), BF),
            pltpu.VMEM((NX, 8, *tall), BF),
            pltpu.VMEM((NX, ROWS, D), BF),
            pltpu.VMEM((NX, ROWS, D), BF),
            pltpu.VMEM((NX, ROWS, D), BF),
            pltpu.VMEM((NZ, NX * SLOTS, PAIR), BF),
            pltpu.VMEM((NZ, 8, PAIR), F32),
            pltpu.VMEM((NX, NY, 2, *two), BF),
            pltpu.VMEM((NX, NY, 2, *tall), BF),
            pltpu.VMEM((NZ, TOK, D), BF),
            pltpu.VMEM((NZ, TOK, D), BF),
            pltpu.VMEM((NZ, TOP, TOK), F32),
            pltpu.VMEM((14, TOK, D), BF),
            pltpu.VMEM((14, TOP, TOK), F32),
            pltpu.VMEM((NZ, NC, TOP, TOK), F32),
            *[pltpu.VMEM((2, 2, *s), BF) for s in (two, tall)],
            *[pltpu.VMEM((2, 4, *s), BF) for s in (two, tall)],
            *[pltpu.VMEM((4, *s), BF) for s in (two, tall)],
            *[pltpu.VMEM((4, 2, *s), BF) for s in (two, tall)],
            *[pltpu.VMEM((2, 3, *s), BF) for s in (two, tall)],
            *[pltpu.VMEM((2, *s), BF) for s in (two, tall)],
            pltpu.SemaphoreType.DMA((N_SEND,)),
            pltpu.SemaphoreType.DMA((N_RECV,)),
            pltpu.SemaphoreType.DMA((5,)),
        ],
        compiler_params=pltpu.CompilerParams(
            collective_id=0,
            has_side_effects=True,
            vmem_limit_bytes=60 * 1024 * 1024,
        ),
    )(tokens, out_grad, expert_ids.T, route_weights.T, gate_weight, up_weight, down_weight)
    layer_out, token_grad, route_grad, gate_share, up_share, down_share = pl.pallas_call(
        hand_out,
        out_shape=out_shape,
        in_specs=[vmem] * 6,
        out_specs=(vmem,) * 6,
    )(*results)
    return (layer_out, token_grad, route_grad.T, gate_share, up_share, down_share)


def solution(mesh):
    return jax.shard_map(
        per_device,
        mesh=mesh,
        in_specs=(
            P(("rep", "ep"), None),
            P(("rep", "ep"), None),
            P(("rep", "ep"), None),
            P(("rep", "ep"), None),
            P("ep", None, None),
            P("ep", None, None),
            P("ep", None, None),
        ),
        out_specs=(
            P(("rep", "ep"), None),
            P(("rep", "ep"), None),
            P(("rep", "ep"), None),
            P("ep", "rep", None),
            P("ep", "rep", None),
            P("ep", "rep", None),
        ),
        check_vma=False,
    )
```

```python
import jax
import jax.numpy as jnp
from jax import lax
from jax.experimental import pallas as pl
from jax.experimental.pallas import tpu as pltpu
from jax.sharding import PartitionSpec as P

MESH = pl.DeviceIdType.MESH
NX, NY, NZ, NC = 4, 4, 8, 2
TOK, D, FF, TOP, CAP = 128, 1024, 384, 8, 24
PAIR = 2 * TOK
SLOTS = 2 * CAP
ROWS = NZ * SLOTS
BF = jnp.bfloat16
F32 = jnp.float32


def nn(a, b):
    return lax.dot_general(a, b, (((1,), (0,)), ((), ())), preferred_element_type=F32)


def nt(a, b):
    return lax.dot_general(a, b, (((1,), (1,)), ((), ())), preferred_element_type=F32)


def tn(a, b):
    return lax.dot_general(a, b, (((0,), (0,)), ((), ())), preferred_element_type=F32)


class Net:
    def __init__(self, send, recv):
        self.send_sems, self.recv_sems = send, recv
        self.sent = self.count = 0
        self.pending = []

    def copy(self, src, dst, dev, out, into):
        return pltpu.make_async_remote_copy(
            src_ref=src,
            dst_ref=dst,
            send_sem=self.send_sems.at[out],
            recv_sem=self.recv_sems.at[into],
            device_id=dev,
            device_id_type=MESH,
        )

    def put(self, src, dst, dev):
        copy = self.copy(src, dst, dev, self.sent, self.count)
        copy.start()
        self.pending.append(copy)
        self.sent, self.count = self.sent + 1, self.count + 1
        return self.count - 1, dev

    def got(self, ticket, dst):
        into, dev = ticket
        self.copy(dst, dst, dev, 0, into).wait_recv()

    def drain(self):
        for copy in self.pending:
            copy.wait_send()
        self.pending, self.sent = [], 0


N_SEND, N_RECV = 99, 194
SIGNS = (1, -1)
LAST = ((4, 3), (3, 4))


def kernel(
    tok, grd, ids_in, weights_in, gw, uw, dw,
    lo, tg, rg, go, uo, do,
    tok_all, grd_all, meta_all, wg, wu, wd, xs, ors, igs, pts, w8s,
    gx, gd, sib_l, sib_t, sib_r, rz, zr, rp,
    xfx, xfd, xnx, xnd, yfx, yfd, ynx, ynd, sx, sd, hx, hd,
    send_sems, recv_sems, local_sems,
):
    rep, ep = lax.axis_index("rep"), lax.axis_index("ep")
    y, c = lax.div(rep, NC), lax.rem(rep, NC)
    x, z = lax.div(ep, NZ), lax.rem(ep, NZ)

    def up_x(d):
        return lax.rem(x + d + NX, NX)

    def up_y(d):
        return lax.rem(y + d + NY, NY)

    def up_z(d):
        return lax.rem(z + d + NZ, NZ)

    def dev(dx=0, dy=0, dz=0, dc=0):
        return (
            up_y(dy) * NC + lax.rem(c + dc, NC),
            up_x(dx) * NZ + up_z(dz),
        )

    sib = dev(dc=1)
    other = lax.rem(c + 1, NC)
    barrier = pltpu.get_barrier_semaphore()
    partners = [sib, dev(dx=1), dev(dx=-1), dev(dy=1), dev(dy=-1), dev(dz=1), dev(dz=-1)]
    for partner in partners:
        pl.semaphore_signal(barrier, inc=1, device_id=partner, device_id_type=MESH)
    meta_all[z, c, 0:8] = ids_in[...].astype(F32)
    meta_all[z, c, 8:16] = weights_in[...]
    pl.semaphore_wait(barrier, len(partners))
    net = Net(send_sems, recv_sems)

    blocks = (tok_all, grd_all)
    firsts = (tok, grd)
    ring, sibs = {}, {}

    def z_send(way, a, s):
        d = SIGNS[way]
        block = blocks[a].at[up_z(-d * s), c]
        src = firsts[a] if s == 0 else block
        ring[way, a, s] = net.put(src, block, dev(dz=d))
        if a == 0:
            note = meta_all.at[up_z(-d * s), c]
            ring[way, 2, s] = net.put(note, note, dev(dz=d))

    def z_step(a, s):
        for way in range(2):
            if s < LAST[way][a]:
                off = -SIGNS[way] * (s + 1)
                where = up_z(off)
                block = blocks[a].at[where, c]
                net.got(ring[way, a, s], block)
                if a == 0:
                    net.got(ring[way, 2, s], meta_all.at[where, c])
                if s + 1 < LAST[way][a]:
                    z_send(way, a, s + 1)
                share(a, off, block)

    def share(a, off, src):
        where = up_z(off)
        sibs[a, off % NZ] = net.put(src, blocks[a].at[where, c], sib)
        if a == 0:
            note = meta_all.at[where, c]
            sibs[2, off % NZ] = net.put(note, note, sib)

    for a in range(2):
        for way in range(2):
            z_send(way, a, 0)
    rings_x = {}

    def x_send(name, way, s, src, dst):
        rings_x[name, way, s] = net.put(src, dst, dev(dx=SIGNS[way]))

    quarter = ((uw, wu), (dw, wd))
    for h in range(2):
        for m in range(2):
            for way in range(2):
                x_send((m, h), way, 0, quarter[m][0].at[c, 2 * y + h], quarter[m][1].at[x, 2 * y + h])
    for a in range(2):
        share(a, 0, firsts[a])
    local = [
        pltpu.make_async_copy(src, dst, local_sems.at[i])
        for i, (src, dst) in enumerate(
            (
                (tok, tok_all.at[z, c]),
                (grd, grd_all.at[z, c]),
                (gw.at[c], wg.at[x]),
                (uw.at[c], wu.at[x]),
                (dw.at[c], wd.at[x]),
            )
        )
    ]
    for copy in local:
        copy.start()

    rings_y = {}

    def y_send(name, way, s, ref):
        rings_y[name, way, s] = net.put(ref, ref, dev(dy=SIGNS[way]))

    def x_take_quarters(way):
        d = SIGNS[way]
        for h in range(2):
            for m in range(2):
                piece = quarter[m][1].at[up_x(-d), 2 * y + h]
                net.got(rings_x[(m, h), way, 0], piece)
                if h == way:
                    x_send((m, h), way, 1, piece, piece)
                for to in range(2):
                    y_send((m, h, -d), to, 0, piece)

    def x_take_far():
        for m in range(2):
            for way in range(2):
                piece = quarter[m][1].at[up_x(2), 2 * y + way]
                net.got(rings_x[(m, way), way, 1], piece)
                for to in range(2):
                    y_send((m, way, 2), to, 0, piece)

    def y_take(dx):
        for m in range(2):
            for way in range(2):
                for h in range(2):
                    piece = quarter[m][1].at[up_x(dx), 2 * up_y(-SIGNS[way]) + h]
                    net.got(rings_y[(m, h, dx), way, 0], piece)
                    if h == way:
                        y_send((m, h, dx), way, 1, piece)

    def y_take_far(dx):
        for m in range(2):
            for way in range(2):
                piece = quarter[m][1].at[up_x(dx), 2 * up_y(2) + way]
                net.got(rings_y[(m, way, dx), way, 1], piece)

    def x_take_gate():
        for way in range(2):
            for h in range(2):
                piece = wg.at[up_x(-SIGNS[way]), pl.ds(4 * h, 4)]
                net.got(rings_x[(2, h), way, 0], piece)
                if h == way:
                    x_send((2, h), way, 1, piece, piece)

    def x_take_gate_far():
        for way in range(2):
            piece = wg.at[up_x(2), pl.ds(4 * way, 4)]
            net.got(rings_x[(2, way), way, 1], piece)

    expert_col = lax.broadcasted_iota(jnp.int32, (8, PAIR), 0)
    names = jnp.where(expert_col < NX, 2 * (expert_col * NZ + z) + c, -1).astype(F32)
    t_row = lax.broadcasted_iota(jnp.int32, (PAIR, PAIR), 0)
    t_col = lax.broadcasted_iota(jnp.int32, (PAIR, PAIR), 1)
    same = (t_row < TOK) == (t_col < TOK)
    earlier = jnp.where((t_row < t_col) & same, 1.0, 0.0).astype(BF)
    base = jnp.where(lax.broadcasted_iota(jnp.int32, (8, PAIR), 1) < TOK, 0.0, float(CAP))
    slot_no = lax.broadcasted_iota(jnp.int32, (SLOTS, PAIR), 0).astype(F32)

    def ids_of(p):
        return jnp.concatenate([meta_all[p, 0, 0:8], meta_all[p, 1, 0:8]], axis=1)

    def pack(off):
        p = up_z(off)
        for a in range(2):
            net.got(sibs[a, off % NZ], blocks[a].at[p, other])
        net.got(sibs[2, off % NZ], meta_all.at[p, other])
        ids = ids_of(p)
        weights = jnp.concatenate([meta_all[p, 0, 8:16], meta_all[p, 1, 8:16]], axis=1)
        hot, w8 = jnp.zeros((8, PAIR), F32), jnp.zeros((8, PAIR), F32)
        for k in range(TOP):
            hit = ids[k : k + 1] == names
            hot = hot + jnp.where(hit, 1.0, 0.0)
            w8 = w8 + jnp.where(hit, weights[k : k + 1], 0.0)
        rank = nn(hot.astype(BF), earlier)
        slot = jnp.where(hot > 0.5, rank + base, -1.0)
        rows, scales = [], []
        for i in range(NX):
            one = jnp.where(slot[i : i + 1] == slot_no, 1.0, 0.0)
            rows.append(one)
            scales.append(jnp.sum(one * w8[i : i + 1], axis=1, keepdims=True))
        pt = jnp.concatenate(rows, axis=0).astype(BF)
        scale = jnp.concatenate(scales, axis=0)
        pts[p] = pt
        w8s[p] = w8
        at = pl.ds(pl.multiple_of(p * SLOTS, 16), SLOTS)
        packed = nn(pt, tok_all[p].reshape(PAIR, D)).astype(BF)
        xs[:, at, :] = packed.reshape(NX, SLOTS, D)
        scaled = (nn(pt, grd_all[p].reshape(PAIR, D)) * scale).astype(BF)
        ors[:, at, :] = scaled.reshape(NX, SLOTS, D)

    def expert(dx, early=False):
        i = up_x(dx)
        gate_w, up_w = wg[i].reshape(D, FF), wu[i].reshape(D, FF)
        down_w = wd[i].reshape(FF, D)
        rows, outs = xs[i], ors[i]
        gate_pre, up_pre = nn(rows, gate_w), nn(rows, up_w)
        sig = jax.nn.sigmoid(gate_pre)
        silu = gate_pre * sig
        slope = sig * (1.0 + gate_pre * (1.0 - sig))
        hidden = (silu * up_pre).astype(BF)
        if early:
            gd[i] = tn(hidden, outs).astype(BF).reshape(NY, 2, FF // 8, D)
            grad_send(dx, 1)
        hidden_grad = nt(outs, down_w)
        gate_delta = (hidden_grad * up_pre * slope).astype(BF)
        up_delta = (hidden_grad * silu).astype(BF)
        if early:
            for m, delta in enumerate((gate_delta, up_delta)):
                gx[i, :, :, m] = tn(rows, delta).astype(BF).reshape(NY, 2, TOK, FF)
            grad_send(dx, 0)
        igs[i] = (nt(gate_delta, gate_w) + nt(up_delta, up_w)).astype(BF)
        expert_out = nn(hidden, down_w).astype(BF)
        wd[i] = expert_out.reshape(8, ROWS // 8, D)
        if not early:
            wg[i, 0:3] = hidden.reshape(3, TOK, FF)
            wu[i, 0:3] = gate_delta.reshape(3, TOK, FF)
            wu[i, 3:6] = up_delta.reshape(3, TOK, FF)

    def weight_grads(dx):
        i = up_x(dx)
        rows, outs = xs[i], ors[i]
        for m in range(2):
            delta = wu[i, 3 * m : 3 * m + 3].reshape(ROWS, FF)
            gx[i, :, :, m] = tn(rows, delta).astype(BF).reshape(NY, 2, TOK, FF)
        hidden = wg[i, 0:3].reshape(ROWS, FF)
        gd[i] = tn(hidden, outs).astype(BF).reshape(NY, 2, FF // 8, D)

    parts = (tok_all, grd_all)
    sib_bufs = (sib_l, sib_t)
    sib_tickets = {}

    def combine(off):
        p = up_z(off)
        ids = ids_of(p)
        pt, w8 = pts[p].astype(F32), w8s[p]
        outs = wd[:, p].reshape(NX * SLOTS, D)
        at = pl.ds(pl.multiple_of(p * SLOTS, 16), SLOTS)
        ins = igs[:, at, :].reshape(NX * SLOTS, D)
        weighted = jnp.concatenate(
            [pt[i * SLOTS : (i + 1) * SLOTS] * w8[i : i + 1] for i in range(NX)], axis=0
        ).astype(BF)
        dots = nt(outs, grd_all[p].reshape(PAIR, D)) * pt
        route = jnp.zeros((8, PAIR), F32)
        for i in range(NX):
            value = jnp.sum(dots[i * SLOTS : (i + 1) * SLOTS], axis=0, keepdims=True)
            route = route + jnp.where(ids == names[i : i + 1], value, 0.0)
        rp[p, 0] = route[:, :TOK]
        rp[p, 1] = route[:, TOK:]
        tok_all[p] = tn(weighted, outs).astype(BF).reshape(2, TOK, D)
        grd_all[p] = tn(pts[p], ins).astype(BF).reshape(2, TOK, D)
        for a in range(2):
            sib_tickets[a, off % NZ] = net.put(parts[a].at[p, other], sib_bufs[a].at[p], sib)
        sib_tickets[2, off % NZ] = net.put(rp.at[p, other], sib_r.at[p], sib)

    x_take_quarters(0)
    x_take_quarters(1)
    for h in range(2):
        for way in range(2):
            part = pl.ds(4 * h, 4)
            x_send((2, h), way, 0, gw.at[c, part], wg.at[x, part])
    z_step(0, 0)
    for copy in local:
        copy.wait()
    z_step(1, 0)
    x_take_far()
    pack(0)
    z_step(0, 1)
    y_take(-1)
    pack(1)
    pack(-1)
    z_step(1, 1)
    y_take(1)
    z_step(0, 2)
    x_take_gate()
    y_take(2)
    pack(2)
    pack(-2)
    z_step(1, 2)
    y_take_far(-1)
    y_take_far(1)
    z_step(0, 3)
    pack(3)
    pack(-3)
    z_step(1, 3)
    y_take_far(2)
    x_take_gate_far()
    pack(4)
    net.drain()

    grads = (gx, gd)
    chain, tickets = {}, {}
    buf_no = {}
    for way in range(2):
        for a in range(2):
            for s in range(LAST[way][a]):
                buf_no[way, a, s] = len(buf_no)

    def add(ref, *more):
        total = ref[...].astype(F32)
        for m in more:
            total = total + m[...].astype(F32)
        ref[...] = total.astype(BF)

    def z_pass(way, a, s):
        d = SIGNS[way]
        off = d * (LAST[way][a] - s)
        where = up_z(off)
        net.got(sib_tickets[a, off % NZ], sib_bufs[a].at[where])
        block = parts[a].at[where, c]
        more = [sib_bufs[a].at[where]]
        if s > 0:
            came = rz.at[buf_no[way, a, s - 1]]
            net.got(chain[way, a, s - 1], came)
            more.append(came)
        add(block, *more)
        chain[way, a, s] = net.put(block, rz.at[buf_no[way, a, s]], dev(dz=d))
        if a == 0:
            net.got(sib_tickets[2, off % NZ], sib_r.at[where])
            route = rp[where, c] + sib_r[where]
            if s > 0:
                net.got(chain[way, 2, s - 1], zr.at[buf_no[way, 0, s - 1]])
                route = route + zr[buf_no[way, 0, s - 1]]
            rp[where, c] = route
            chain[way, 2, s] = net.put(
                rp.at[where, c], zr.at[buf_no[way, 0, s]], dev(dz=d)
            )

    half = (pl.ds(0, 2), pl.ds(2, 2))
    far_x, near_x = (xfx, xfd), (xnx, xnd)
    far_y, near_y = (yfx, yfd), (ynx, ynd)
    second = (sx, sd)

    def y_way(dx):
        return 0 if dx in (2, -1) else 1

    def grad_send(dx, *which):
        i = up_x(dx)
        for g in which:
            if dx == 2:
                for way in range(2):
                    tickets["xf", way, g] = net.put(
                        grads[g].at[i, half[way], 0], far_x[g].at[way], dev(dx=SIGNS[way])
                    )
            way = y_way(dx)
            tickets["yf", dx, g] = net.put(
                grads[g].at[i, up_y(2), 1], far_y[g].at[dx % NX], dev(dy=SIGNS[way])
            )
            tickets["yn", dx, 1 - way, g] = net.put(
                grads[g].at[i, up_y(SIGNS[1 - way]), 1],
                near_y[g].at[dx % NX, 1 - way],
                dev(dy=SIGNS[1 - way]),
            )

    def x_pass(way):
        i = up_x(SIGNS[way])
        for g in range(2):
            net.got(tickets["xf", way, g], far_x[g].at[way])
            mine = grads[g].at[i, half[way], 0]
            add(mine, far_x[g].at[way])
            tickets["xb", way, g] = net.put(
                mine, near_x[g].at[way, half[way]], dev(dx=SIGNS[way])
            )
            free = half[1 - way]
            tickets["xa", way, g] = net.put(
                grads[g].at[i, free, 0], near_x[g].at[way, free], dev(dx=SIGNS[way])
            )

    def y_pass(dx):
        way = y_way(dx)
        for g in range(2):
            net.got(tickets["yf", dx, g], far_y[g].at[dx % NX])
            mine = grads[g].at[up_x(dx), up_y(SIGNS[way]), 1]
            add(mine, far_y[g].at[dx % NX])
            tickets["yn", dx, way, g] = net.put(
                mine, near_y[g].at[dx % NX, way], dev(dy=SIGNS[way])
            )

    def second_view(h, g, d):
        return grads[g].at[x, up_y(d), 0] if h == 0 else grads[g].at[up_x(d), y, 1]

    def second_dev(h, way):
        return dev(dy=SIGNS[way]) if h == 0 else dev(dx=SIGNS[way])

    def far_send(h, g):
        tickets["sf", h, g] = net.put(
            second_view(h, g, 2), second[g].at[h, 2], second_dev(h, g)
        )

    def near_send(h, g):
        way = 1 - g
        tickets["sn", h, g, way] = net.put(
            second_view(h, g, SIGNS[way]), second[g].at[h, way], second_dev(h, way)
        )

    def x_last():
        for g in range(2):
            for way in range(2):
                net.got(tickets["xa", way, g], near_x[g].at[way, half[1 - way]])
                net.got(tickets["xb", way, g], near_x[g].at[way, half[way]])
            add(grads[g].at[x, :, 0], near_x[g].at[0], near_x[g].at[1])
            far_send(0, g)
            near_send(0, g)

    def y_last(dx):
        for g in range(2):
            for way in range(2):
                net.got(tickets["yn", dx, way, g], near_y[g].at[dx % NX, way])
            near = near_y[g].at[dx % NX]
            add(grads[g].at[up_x(dx), y, 1], near.at[0], near.at[1])
            if dx == 2:
                far_send(1, g)
            elif dx == SIGNS[1 - g]:
                near_send(1, g)

    def second_pass(h):
        for g in range(2):
            way = g
            net.got(tickets["sf", h, g], second[g].at[h, 2])
            mine = second_view(h, g, SIGNS[way])
            add(mine, second[g].at[h, 2])
            tickets["sn", h, g, way] = net.put(
                mine, second[g].at[h, way], second_dev(h, way)
            )

    expert(2, early=True)
    expert(1, early=True)
    expert(-1)
    expert(0)
    combine(4)
    combine(3)
    combine(-3)
    y_pass(2)
    z_pass(0, 0, 0)
    z_pass(1, 1, 0)
    z_pass(0, 1, 0)
    z_pass(1, 0, 0)
    x_pass(0)
    weight_grads(-1)
    grad_send(-1, 0, 1)
    x_pass(1)
    y_pass(1)
    weight_grads(0)
    grad_send(0, 0, 1)
    combine(2)
    combine(-2)
    z_pass(0, 0, 1)
    z_pass(1, 1, 1)
    z_pass(0, 1, 1)
    z_pass(1, 0, 1)
    y_pass(-1)
    combine(1)
    combine(-1)
    y_pass(0)
    y_last(2)
    z_pass(0, 0, 2)
    z_pass(1, 1, 2)
    y_last(1)
    z_pass(0, 1, 2)
    z_pass(1, 0, 2)
    combine(0)
    y_last(-1)
    x_last()
    second_pass(1)
    z_pass(0, 0, 3)
    z_pass(1, 1, 3)
    y_last(0)
    second_pass(0)

    results = (lo, tg)
    for a in range(2):
        net.got(sib_tickets[a, 0], sib_bufs[a].at[z])
        total = parts[a][z, c].astype(F32) + sib_bufs[a][z].astype(F32)
        for way in range(2):
            s = LAST[way][a] - 1
            came = rz.at[buf_no[way, a, s]]
            net.got(chain[way, a, s], came)
            total = total + came[...].astype(F32)
        results[a][...] = total.astype(BF)
    net.got(sib_tickets[2, 0], sib_r.at[z])
    total = rp[z, c] + sib_r[z]
    for way in range(2):
        no = buf_no[way, 0, LAST[way][0] - 1]
        net.got(chain[way, 2, LAST[way][0] - 1], zr.at[no])
        total = total + zr[no]
    rg[...] = total

    finals = ((go, uo), (do,))
    stage = (hx, hd)
    hand = []
    for g in range(2):
        both = []
        for h in range(2):
            for way in range(2):
                net.got(tickets["sn", h, g, way], second[g].at[h, way])
            both.append(
                second_view(h, g, 0)[...].astype(F32)
                + second[g][h, 0].astype(F32)
                + second[g][h, 1].astype(F32)
            )
        keep = jnp.where(c == 0, both[0], both[1])
        away = jnp.where(c == 0, both[1], both[0])
        stage[g][0] = away.astype(BF)
        hand.append(net.put(stage[g].at[0], stage[g].at[1], sib))
        if g == 0:
            go[c], uo[c] = keep[0], keep[1]
        else:
            do[c] = keep
    net.got(hand[0], hx.at[1])
    go[other] = hx[1, 0].astype(F32)
    uo[other] = hx[1, 1].astype(F32)
    net.got(hand[1], hd.at[1])
    do[other] = hd[1].astype(F32)
    net.drain()


def hand_out(*refs):
    n = len(refs) // 2
    for i in range(n):
        refs[n + i][...] = refs[i][...]


def per_device(tokens, expert_ids, route_weights, out_grad, gate_weight, up_weight, down_weight):
    gate_weight = gate_weight.reshape(2, 8, D // 8, FF)
    up_weight = up_weight.reshape(2, 8, D // 8, FF)
    down_weight = down_weight.reshape(2, 8, FF // 8, D)
    vmem = pl.BlockSpec(memory_space=pltpu.VMEM)
    hbm = pl.BlockSpec(memory_space=pl.ANY)
    wide, tall = (D // 8, FF), (FF // 8, D)
    two = (2, *wide)
    out_shape = (
        jax.ShapeDtypeStruct((TOK, D), BF),
        jax.ShapeDtypeStruct((TOK, D), BF),
        jax.ShapeDtypeStruct((TOP, TOK), F32),
        jax.ShapeDtypeStruct((2, *wide), F32),
        jax.ShapeDtypeStruct((2, *wide), F32),
        jax.ShapeDtypeStruct((2, *tall), F32),
    )
    results = pl.pallas_call(
        kernel,
        out_shape=out_shape,
        in_specs=[hbm, hbm, vmem, vmem, hbm, hbm, hbm],
        out_specs=(vmem,) * 6,
        scratch_shapes=[
            pltpu.VMEM((NZ, NC, TOK, D), BF),
            pltpu.VMEM((NZ, NC, TOK, D), BF),
            pltpu.VMEM((NZ, NC, 16, TOK), F32),
            pltpu.VMEM((NX, 8, *wide), BF),
            pltpu.VMEM((NX, 8, *wide), BF),
            pltpu.VMEM((NX, 8, *tall), BF),
            pltpu.VMEM((NX, ROWS, D), BF),
            pltpu.VMEM((NX, ROWS, D), BF),
            pltpu.VMEM((NX, ROWS, D), BF),
            pltpu.VMEM((NZ, NX * SLOTS, PAIR), BF),
            pltpu.VMEM((NZ, 8, PAIR), F32),
            pltpu.VMEM((NX, NY, 2, *two), BF),
            pltpu.VMEM((NX, NY, 2, *tall), BF),
            pltpu.VMEM((NZ, TOK, D), BF),
            pltpu.VMEM((NZ, TOK, D), BF),
            pltpu.VMEM((NZ, TOP, TOK), F32),
            pltpu.VMEM((14, TOK, D), BF),
            pltpu.VMEM((14, TOP, TOK), F32),
            pltpu.VMEM((NZ, NC, TOP, TOK), F32),
            *[pltpu.VMEM((2, 2, *s), BF) for s in (two, tall)],
            *[pltpu.VMEM((2, 4, *s), BF) for s in (two, tall)],
            *[pltpu.VMEM((4, *s), BF) for s in (two, tall)],
            *[pltpu.VMEM((4, 2, *s), BF) for s in (two, tall)],
            *[pltpu.VMEM((2, 3, *s), BF) for s in (two, tall)],
            *[pltpu.VMEM((2, *s), BF) for s in (two, tall)],
            pltpu.SemaphoreType.DMA((N_SEND,)),
            pltpu.SemaphoreType.DMA((N_RECV,)),
            pltpu.SemaphoreType.DMA((5,)),
        ],
        compiler_params=pltpu.CompilerParams(
            collective_id=0,
            has_side_effects=True,
            vmem_limit_bytes=63 * 1024 * 1024,
        ),
    )(tokens, out_grad, expert_ids.T, route_weights.T, gate_weight, up_weight, down_weight)
    layer_out, token_grad, route_grad, gate_share, up_share, down_share = pl.pallas_call(
        hand_out,
        out_shape=out_shape,
        in_specs=[vmem] * 6,
        out_specs=(vmem,) * 6,
    )(*results)
    return (layer_out, token_grad, route_grad.T, gate_share, up_share, down_share)


def solution(mesh):
    return jax.shard_map(
        per_device,
        mesh=mesh,
        in_specs=(
            P(("rep", "ep"), None),
            P(("rep", "ep"), None),
            P(("rep", "ep"), None),
            P(("rep", "ep"), None),
            P("ep", None, None),
            P("ep", None, None),
            P("ep", None, None),
        ),
        out_specs=(
            P(("rep", "ep"), None),
            P(("rep", "ep"), None),
            P(("rep", "ep"), None),
            P("ep", "rep", None),
            P("ep", "rep", None),
            P("ep", "rep", None),
        ),
        check_vma=False,
    )
```

```python
import jax
import jax.numpy as jnp
from jax import lax
from jax.experimental import pallas as pl
from jax.experimental.pallas import tpu as pltpu
from jax.sharding import PartitionSpec as P

MESH = pl.DeviceIdType.MESH
NX, NY, NZ, NC = 4, 4, 8, 2
TOK, D, FF, TOP, CAP = 128, 1024, 384, 8, 24
PAIR = 2 * TOK
SLOTS = 2 * CAP
ROWS = NZ * SLOTS
BF = jnp.bfloat16
F32 = jnp.float32


def nn(a, b):
    return lax.dot_general(a, b, (((1,), (0,)), ((), ())), preferred_element_type=F32)


def nt(a, b):
    return lax.dot_general(a, b, (((1,), (1,)), ((), ())), preferred_element_type=F32)


def tn(a, b):
    return lax.dot_general(a, b, (((0,), (0,)), ((), ())), preferred_element_type=F32)


class Net:
    def __init__(self, send, recv):
        self.send_sems, self.recv_sems = send, recv
        self.sent = self.count = 0
        self.pending = []

    def copy(self, src, dst, dev, out, into):
        return pltpu.make_async_remote_copy(
            src_ref=src,
            dst_ref=dst,
            send_sem=self.send_sems.at[out],
            recv_sem=self.recv_sems.at[into],
            device_id=dev,
            device_id_type=MESH,
        )

    def put(self, src, dst, dev):
        copy = self.copy(src, dst, dev, self.sent, self.count)
        copy.start()
        self.pending.append(copy)
        self.sent, self.count = self.sent + 1, self.count + 1
        return self.count - 1, dev

    def got(self, ticket, dst):
        into, dev = ticket
        self.copy(dst, dst, dev, 0, into).wait_recv()

    def drain(self):
        for copy in self.pending:
            copy.wait_send()
        self.pending, self.sent = [], 0


N_SEND, N_RECV = 95, 180
SIGNS = (1, -1)
LAST = ((4, 3), (3, 4))


def kernel(
    tok, grd, ids_in, weights_in, gw, uw, dw,
    lo, tg, rg, go, uo, do,
    tok_all, grd_all, meta_all, wg, wu, wd, xs, ors, igs, pts, w8s,
    gx, gd, sib_l, sib_t, sib_r, rz, zr, rp,
    xfx, xfd, xnx, xnd, yfx, yfd, ynx, ynd, sx, sd, hx, hd,
    send_sems, recv_sems, local_sems,
):
    rep, ep = lax.axis_index("rep"), lax.axis_index("ep")
    y, c = lax.div(rep, NC), lax.rem(rep, NC)
    x, z = lax.div(ep, NZ), lax.rem(ep, NZ)

    def up_x(d):
        return lax.rem(x + d + NX, NX)

    def up_y(d):
        return lax.rem(y + d + NY, NY)

    def up_z(d):
        return lax.rem(z + d + NZ, NZ)

    def dev(dx=0, dy=0, dz=0, dc=0):
        return (
            up_y(dy) * NC + lax.rem(c + dc, NC),
            up_x(dx) * NZ + up_z(dz),
        )

    sib = dev(dc=1)
    other = lax.rem(c + 1, NC)
    barrier = pltpu.get_barrier_semaphore()
    partners = [sib, dev(dx=1), dev(dx=-1), dev(dy=1), dev(dy=-1), dev(dz=1), dev(dz=-1)]
    for partner in partners:
        pl.semaphore_signal(barrier, inc=1, device_id=partner, device_id_type=MESH)
    meta_all[z, c, 0:8] = ids_in[...].astype(F32)
    meta_all[z, c, 8:16] = weights_in[...]
    pl.semaphore_wait(barrier, len(partners))
    net = Net(send_sems, recv_sems)

    blocks = (tok_all, grd_all)
    firsts = (tok, grd)
    ring, sibs = {}, {}

    def z_send(way, a, s):
        d = SIGNS[way]
        block = blocks[a].at[up_z(-d * s), c]
        src = firsts[a] if s == 0 else block
        ring[way, a, s] = net.put(src, block, dev(dz=d))
        if a == 0:
            note = meta_all.at[up_z(-d * s), c]
            ring[way, 2, s] = net.put(note, note, dev(dz=d))

    def z_step(a, s):
        for way in range(2):
            if s < LAST[way][a]:
                off = -SIGNS[way] * (s + 1)
                where = up_z(off)
                block = blocks[a].at[where, c]
                net.got(ring[way, a, s], block)
                if a == 0:
                    net.got(ring[way, 2, s], meta_all.at[where, c])
                if s + 1 < LAST[way][a]:
                    z_send(way, a, s + 1)
                share(a, off, block)

    def share(a, off, src):
        where = up_z(off)
        sibs[a, off % NZ] = net.put(src, blocks[a].at[where, c], sib)
        if a == 0:
            note = meta_all.at[where, c]
            sibs[2, off % NZ] = net.put(note, note, sib)

    for a in range(2):
        for way in range(2):
            z_send(way, a, 0)
    rings_x = {}

    def x_send(name, way, s, src, dst):
        rings_x[name, way, s] = net.put(src, dst, dev(dx=SIGNS[way]))

    quarter = ((uw, wu), (dw, wd))
    mine = pl.ds(2 * y, 2)
    for m in range(2):
        for way in range(2):
            x_send(m, way, 0, quarter[m][0].at[c, mine], quarter[m][1].at[x, mine])
    for a in range(2):
        share(a, 0, firsts[a])
    local = [
        pltpu.make_async_copy(src, dst, local_sems.at[i])
        for i, (src, dst) in enumerate(
            (
                (tok, tok_all.at[z, c]),
                (grd, grd_all.at[z, c]),
                (gw.at[c], wg.at[x]),
                (uw.at[c], wu.at[x]),
                (dw.at[c], wd.at[x]),
            )
        )
    ]
    for copy in local:
        copy.start()

    rings_y = {}

    def y_send(name, way, s, ref):
        rings_y[name, way, s] = net.put(ref, ref, dev(dy=SIGNS[way]))

    def x_take_quarters(way):
        d = SIGNS[way]
        for m in range(2):
            both = quarter[m][1].at[up_x(-d), mine]
            net.got(rings_x[m, way, 0], both)
            piece = quarter[m][1].at[up_x(-d), 2 * y + way]
            x_send((m, way), way, 1, piece, piece)
            for to in range(2):
                y_send((m, -d), to, 0, both)

    def x_take_far():
        for m in range(2):
            for way in range(2):
                piece = quarter[m][1].at[up_x(2), 2 * y + way]
                net.got(rings_x[(m, way), way, 1], piece)
                for to in range(2):
                    y_send((m, way, 2), to, 0, piece)

    def y_take(dx):
        for m in range(2):
            for way in range(2):
                first = 2 * up_y(-SIGNS[way])
                if dx != 2:
                    both = quarter[m][1].at[up_x(dx), pl.ds(first, 2)]
                    net.got(rings_y[(m, dx), way, 0], both)
                for h in range(2):
                    piece = quarter[m][1].at[up_x(dx), first + h]
                    if dx == 2:
                        net.got(rings_y[(m, h, dx), way, 0], piece)
                    if h == way:
                        y_send((m, h, dx), way, 1, piece)

    def y_take_far(dx):
        for m in range(2):
            for way in range(2):
                piece = quarter[m][1].at[up_x(dx), 2 * up_y(2) + way]
                net.got(rings_y[(m, way, dx), way, 1], piece)

    def x_take_gate():
        for way in range(2):
            net.got(rings_x[2, way, 0], wg.at[up_x(-SIGNS[way])])
            piece = wg.at[up_x(-SIGNS[way]), pl.ds(4 * way, 4)]
            x_send((2, way), way, 1, piece, piece)

    def x_take_gate_far():
        for way in range(2):
            piece = wg.at[up_x(2), pl.ds(4 * way, 4)]
            net.got(rings_x[(2, way), way, 1], piece)

    expert_col = lax.broadcasted_iota(jnp.int32, (8, PAIR), 0)
    names = jnp.where(expert_col < NX, 2 * (expert_col * NZ + z) + c, -1).astype(F32)
    t_row = lax.broadcasted_iota(jnp.int32, (PAIR, PAIR), 0)
    t_col = lax.broadcasted_iota(jnp.int32, (PAIR, PAIR), 1)
    same = (t_row < TOK) == (t_col < TOK)
    earlier = jnp.where((t_row < t_col) & same, 1.0, 0.0).astype(BF)
    base = jnp.where(lax.broadcasted_iota(jnp.int32, (8, PAIR), 1) < TOK, 0.0, float(CAP))
    slot_no = lax.broadcasted_iota(jnp.int32, (SLOTS, PAIR), 0).astype(F32)

    def ids_of(p):
        return jnp.concatenate([meta_all[p, 0, 0:8], meta_all[p, 1, 0:8]], axis=1)

    def pack(off):
        p = up_z(off)
        for a in range(2):
            net.got(sibs[a, off % NZ], blocks[a].at[p, other])
        net.got(sibs[2, off % NZ], meta_all.at[p, other])
        ids = ids_of(p)
        weights = jnp.concatenate([meta_all[p, 0, 8:16], meta_all[p, 1, 8:16]], axis=1)
        hot, w8 = jnp.zeros((8, PAIR), F32), jnp.zeros((8, PAIR), F32)
        for k in range(TOP):
            hit = ids[k : k + 1] == names
            hot = hot + jnp.where(hit, 1.0, 0.0)
            w8 = w8 + jnp.where(hit, weights[k : k + 1], 0.0)
        rank = nn(hot.astype(BF), earlier)
        slot = jnp.where(hot > 0.5, rank + base, -1.0)
        rows, scales = [], []
        for i in range(NX):
            one = jnp.where(slot[i : i + 1] == slot_no, 1.0, 0.0)
            rows.append(one)
            scales.append(jnp.sum(one * w8[i : i + 1], axis=1, keepdims=True))
        pt = jnp.concatenate(rows, axis=0).astype(BF)
        scale = jnp.concatenate(scales, axis=0)
        pts[p] = pt
        w8s[p] = w8
        at = pl.ds(pl.multiple_of(p * SLOTS, 16), SLOTS)
        packed = nn(pt, tok_all[p].reshape(PAIR, D)).astype(BF)
        xs[:, at, :] = packed.reshape(NX, SLOTS, D)
        scaled = (nn(pt, grd_all[p].reshape(PAIR, D)) * scale).astype(BF)
        ors[:, at, :] = scaled.reshape(NX, SLOTS, D)

    def expert(dx, early=False):
        i = up_x(dx)
        gate_w, up_w = wg[i].reshape(D, FF), wu[i].reshape(D, FF)
        down_w = wd[i].reshape(FF, D)
        rows, outs = xs[i], ors[i]
        gate_pre, up_pre = nn(rows, gate_w), nn(rows, up_w)
        sig = jax.nn.sigmoid(gate_pre)
        silu = gate_pre * sig
        slope = sig * (1.0 + gate_pre * (1.0 - sig))
        hidden = (silu * up_pre).astype(BF)
        if early:
            gd[i] = tn(hidden, outs).astype(BF).reshape(NY, 2, FF // 8, D)
            grad_send(dx, 1)
        hidden_grad = nt(outs, down_w)
        gate_delta = (hidden_grad * up_pre * slope).astype(BF)
        up_delta = (hidden_grad * silu).astype(BF)
        if early:
            for m, delta in enumerate((gate_delta, up_delta)):
                gx[i, :, :, m] = tn(rows, delta).astype(BF).reshape(NY, 2, TOK, FF)
            grad_send(dx, 0)
        igs[i] = (nt(gate_delta, gate_w) + nt(up_delta, up_w)).astype(BF)
        expert_out = nn(hidden, down_w).astype(BF)
        wd[i] = expert_out.reshape(8, ROWS // 8, D)
        if not early:
            wg[i, 0:3] = hidden.reshape(3, TOK, FF)
            wu[i, 0:3] = gate_delta.reshape(3, TOK, FF)
            wu[i, 3:6] = up_delta.reshape(3, TOK, FF)

    def weight_grads(dx):
        i = up_x(dx)
        rows, outs = xs[i], ors[i]
        for m in range(2):
            delta = wu[i, 3 * m : 3 * m + 3].reshape(ROWS, FF)
            gx[i, :, :, m] = tn(rows, delta).astype(BF).reshape(NY, 2, TOK, FF)
        hidden = wg[i, 0:3].reshape(ROWS, FF)
        gd[i] = tn(hidden, outs).astype(BF).reshape(NY, 2, FF // 8, D)

    parts = (tok_all, grd_all)
    sib_bufs = (sib_l, sib_t)
    sib_tickets = {}

    def combine(off):
        p = up_z(off)
        ids = ids_of(p)
        pt, w8 = pts[p].astype(F32), w8s[p]
        outs = wd[:, p].reshape(NX * SLOTS, D)
        at = pl.ds(pl.multiple_of(p * SLOTS, 16), SLOTS)
        ins = igs[:, at, :].reshape(NX * SLOTS, D)
        weighted = jnp.concatenate(
            [pt[i * SLOTS : (i + 1) * SLOTS] * w8[i : i + 1] for i in range(NX)], axis=0
        ).astype(BF)
        dots = nt(outs, grd_all[p].reshape(PAIR, D)) * pt
        route = jnp.zeros((8, PAIR), F32)
        for i in range(NX):
            value = jnp.sum(dots[i * SLOTS : (i + 1) * SLOTS], axis=0, keepdims=True)
            route = route + jnp.where(ids == names[i : i + 1], value, 0.0)
        rp[p, 0] = route[:, :TOK]
        rp[p, 1] = route[:, TOK:]
        tok_all[p] = tn(weighted, outs).astype(BF).reshape(2, TOK, D)
        grd_all[p] = tn(pts[p], ins).astype(BF).reshape(2, TOK, D)
        for a in range(2):
            sib_tickets[a, off % NZ] = net.put(parts[a].at[p, other], sib_bufs[a].at[p], sib)
        sib_tickets[2, off % NZ] = net.put(rp.at[p, other], sib_r.at[p], sib)

    x_take_quarters(0)
    x_take_quarters(1)
    for way in range(2):
        x_send(2, way, 0, gw.at[c], wg.at[x])
    z_step(0, 0)
    for copy in local:
        copy.wait()
    z_step(1, 0)
    x_take_far()
    pack(0)
    z_step(0, 1)
    y_take(-1)
    pack(1)
    pack(-1)
    z_step(1, 1)
    y_take(1)
    z_step(0, 2)
    x_take_gate()
    y_take(2)
    pack(2)
    pack(-2)
    z_step(1, 2)
    y_take_far(-1)
    y_take_far(1)
    z_step(0, 3)
    pack(3)
    pack(-3)
    z_step(1, 3)
    y_take_far(2)
    x_take_gate_far()
    pack(4)
    net.drain()

    grads = (gx, gd)
    chain, tickets = {}, {}
    buf_no = {}
    for way in range(2):
        for a in range(2):
            for s in range(LAST[way][a]):
                buf_no[way, a, s] = len(buf_no)

    def add(ref, *more):
        total = ref[...].astype(F32)
        for m in more:
            total = total + m[...].astype(F32)
        ref[...] = total.astype(BF)

    def z_pass(way, a, s):
        d = SIGNS[way]
        off = d * (LAST[way][a] - s)
        where = up_z(off)
        net.got(sib_tickets[a, off % NZ], sib_bufs[a].at[where])
        block = parts[a].at[where, c]
        more = [sib_bufs[a].at[where]]
        if s > 0:
            came = rz.at[buf_no[way, a, s - 1]]
            net.got(chain[way, a, s - 1], came)
            more.append(came)
        add(block, *more)
        chain[way, a, s] = net.put(block, rz.at[buf_no[way, a, s]], dev(dz=d))
        if a == 0:
            net.got(sib_tickets[2, off % NZ], sib_r.at[where])
            route = rp[where, c] + sib_r[where]
            if s > 0:
                net.got(chain[way, 2, s - 1], zr.at[buf_no[way, 0, s - 1]])
                route = route + zr[buf_no[way, 0, s - 1]]
            rp[where, c] = route
            chain[way, 2, s] = net.put(
                rp.at[where, c], zr.at[buf_no[way, 0, s]], dev(dz=d)
            )

    half = (pl.ds(0, 2), pl.ds(2, 2))
    far_x, near_x = (xfx, xfd), (xnx, xnd)
    far_y, near_y = (yfx, yfd), (ynx, ynd)
    second = (sx, sd)

    def y_way(dx):
        return 0 if dx in (2, -1) else 1

    def grad_send(dx, *which):
        i = up_x(dx)
        for g in which:
            if dx == 2:
                for way in range(2):
                    tickets["xf", way, g] = net.put(
                        grads[g].at[i, half[way], 0], far_x[g].at[way], dev(dx=SIGNS[way])
                    )
            way = y_way(dx)
            tickets["yf", dx, g] = net.put(
                grads[g].at[i, up_y(2), 1], far_y[g].at[dx % NX], dev(dy=SIGNS[way])
            )
            tickets["yn", dx, 1 - way, g] = net.put(
                grads[g].at[i, up_y(SIGNS[1 - way]), 1],
                near_y[g].at[dx % NX, 1 - way],
                dev(dy=SIGNS[1 - way]),
            )

    def x_pass(way):
        i = up_x(SIGNS[way])
        for g in range(2):
            net.got(tickets["xf", way, g], far_x[g].at[way])
            mine = grads[g].at[i, half[way], 0]
            add(mine, far_x[g].at[way])
            tickets["xb", way, g] = net.put(
                mine, near_x[g].at[way, half[way]], dev(dx=SIGNS[way])
            )
            free = half[1 - way]
            tickets["xa", way, g] = net.put(
                grads[g].at[i, free, 0], near_x[g].at[way, free], dev(dx=SIGNS[way])
            )

    def y_pass(dx):
        way = y_way(dx)
        for g in range(2):
            net.got(tickets["yf", dx, g], far_y[g].at[dx % NX])
            mine = grads[g].at[up_x(dx), up_y(SIGNS[way]), 1]
            add(mine, far_y[g].at[dx % NX])
            tickets["yn", dx, way, g] = net.put(
                mine, near_y[g].at[dx % NX, way], dev(dy=SIGNS[way])
            )

    def second_view(h, g, d):
        return grads[g].at[x, up_y(d), 0] if h == 0 else grads[g].at[up_x(d), y, 1]

    def second_dev(h, way):
        return dev(dy=SIGNS[way]) if h == 0 else dev(dx=SIGNS[way])

    def far_send(h, g):
        tickets["sf", h, g] = net.put(
            second_view(h, g, 2), second[g].at[h, 2], second_dev(h, g)
        )

    def near_send(h, g):
        way = 1 - g
        tickets["sn", h, g, way] = net.put(
            second_view(h, g, SIGNS[way]), second[g].at[h, way], second_dev(h, way)
        )

    def x_last():
        for g in range(2):
            for way in range(2):
                net.got(tickets["xa", way, g], near_x[g].at[way, half[1 - way]])
                net.got(tickets["xb", way, g], near_x[g].at[way, half[way]])
            add(grads[g].at[x, :, 0], near_x[g].at[0], near_x[g].at[1])
            far_send(0, g)
            near_send(0, g)

    def y_last(dx):
        for g in range(2):
            for way in range(2):
                net.got(tickets["yn", dx, way, g], near_y[g].at[dx % NX, way])
            near = near_y[g].at[dx % NX]
            add(grads[g].at[up_x(dx), y, 1], near.at[0], near.at[1])
            if dx == 2:
                far_send(1, g)
            elif dx == SIGNS[1 - g]:
                near_send(1, g)

    def second_pass(h):
        for g in range(2):
            way = g
            net.got(tickets["sf", h, g], second[g].at[h, 2])
            mine = second_view(h, g, SIGNS[way])
            add(mine, second[g].at[h, 2])
            tickets["sn", h, g, way] = net.put(
                mine, second[g].at[h, way], second_dev(h, way)
            )

    expert(2, early=True)
    expert(1, early=True)
    expert(-1)
    expert(0)
    combine(4)
    combine(3)
    combine(-3)
    y_pass(2)
    z_pass(0, 0, 0)
    z_pass(1, 1, 0)
    z_pass(0, 1, 0)
    z_pass(1, 0, 0)
    x_pass(0)
    weight_grads(-1)
    grad_send(-1, 0, 1)
    x_pass(1)
    y_pass(1)
    weight_grads(0)
    grad_send(0, 0, 1)
    combine(2)
    combine(-2)
    z_pass(0, 0, 1)
    z_pass(1, 1, 1)
    z_pass(0, 1, 1)
    z_pass(1, 0, 1)
    y_pass(-1)
    combine(1)
    combine(-1)
    y_pass(0)
    y_last(2)
    z_pass(0, 0, 2)
    z_pass(1, 1, 2)
    y_last(1)
    z_pass(0, 1, 2)
    z_pass(1, 0, 2)
    combine(0)
    y_last(-1)
    x_last()
    second_pass(1)
    z_pass(0, 0, 3)
    z_pass(1, 1, 3)
    y_last(0)
    second_pass(0)

    results = (lo, tg)
    for a in range(2):
        net.got(sib_tickets[a, 0], sib_bufs[a].at[z])
        total = parts[a][z, c].astype(F32) + sib_bufs[a][z].astype(F32)
        for way in range(2):
            s = LAST[way][a] - 1
            came = rz.at[buf_no[way, a, s]]
            net.got(chain[way, a, s], came)
            total = total + came[...].astype(F32)
        results[a][...] = total.astype(BF)
    net.got(sib_tickets[2, 0], sib_r.at[z])
    total = rp[z, c] + sib_r[z]
    for way in range(2):
        no = buf_no[way, 0, LAST[way][0] - 1]
        net.got(chain[way, 2, LAST[way][0] - 1], zr.at[no])
        total = total + zr[no]
    rg[...] = total

    finals = ((go, uo), (do,))
    stage = (hx, hd)
    hand = []
    for g in range(2):
        both = []
        for h in range(2):
            for way in range(2):
                net.got(tickets["sn", h, g, way], second[g].at[h, way])
            both.append(
                second_view(h, g, 0)[...].astype(F32)
                + second[g][h, 0].astype(F32)
                + second[g][h, 1].astype(F32)
            )
        keep = jnp.where(c == 0, both[0], both[1])
        away = jnp.where(c == 0, both[1], both[0])
        stage[g][0] = away.astype(BF)
        hand.append(net.put(stage[g].at[0], stage[g].at[1], sib))
        if g == 0:
            go[c], uo[c] = keep[0], keep[1]
        else:
            do[c] = keep
    net.got(hand[0], hx.at[1])
    go[other] = hx[1, 0].astype(F32)
    uo[other] = hx[1, 1].astype(F32)
    net.got(hand[1], hd.at[1])
    do[other] = hd[1].astype(F32)
    net.drain()


def hand_out(*refs):
    n = len(refs) // 2
    for i in range(n):
        refs[n + i][...] = refs[i][...]


def per_device(tokens, expert_ids, route_weights, out_grad, gate_weight, up_weight, down_weight):
    gate_weight = gate_weight.reshape(2, 8, D // 8, FF)
    up_weight = up_weight.reshape(2, 8, D // 8, FF)
    down_weight = down_weight.reshape(2, 8, FF // 8, D)
    vmem = pl.BlockSpec(memory_space=pltpu.VMEM)
    hbm = pl.BlockSpec(memory_space=pl.ANY)
    wide, tall = (D // 8, FF), (FF // 8, D)
    two = (2, *wide)
    out_shape = (
        jax.ShapeDtypeStruct((TOK, D), BF),
        jax.ShapeDtypeStruct((TOK, D), BF),
        jax.ShapeDtypeStruct((TOP, TOK), F32),
        jax.ShapeDtypeStruct((2, *wide), F32),
        jax.ShapeDtypeStruct((2, *wide), F32),
        jax.ShapeDtypeStruct((2, *tall), F32),
    )
    results = pl.pallas_call(
        kernel,
        out_shape=out_shape,
        in_specs=[hbm, hbm, vmem, vmem, hbm, hbm, hbm],
        out_specs=(vmem,) * 6,
        scratch_shapes=[
            pltpu.VMEM((NZ, NC, TOK, D), BF),
            pltpu.VMEM((NZ, NC, TOK, D), BF),
            pltpu.VMEM((NZ, NC, 16, TOK), F32),
            pltpu.VMEM((NX, 8, *wide), BF),
            pltpu.VMEM((NX, 8, *wide), BF),
            pltpu.VMEM((NX, 8, *tall), BF),
            pltpu.VMEM((NX, ROWS, D), BF),
            pltpu.VMEM((NX, ROWS, D), BF),
            pltpu.VMEM((NX, ROWS, D), BF),
            pltpu.VMEM((NZ, NX * SLOTS, PAIR), BF),
            pltpu.VMEM((NZ, 8, PAIR), F32),
            pltpu.VMEM((NX, NY, 2, *two), BF),
            pltpu.VMEM((NX, NY, 2, *tall), BF),
            pltpu.VMEM((NZ, TOK, D), BF),
            pltpu.VMEM((NZ, TOK, D), BF),
            pltpu.VMEM((NZ, TOP, TOK), F32),
            pltpu.VMEM((14, TOK, D), BF),
            pltpu.VMEM((14, TOP, TOK), F32),
            pltpu.VMEM((NZ, NC, TOP, TOK), F32),
            *[pltpu.VMEM((2, 2, *s), BF) for s in (two, tall)],
            *[pltpu.VMEM((2, 4, *s), BF) for s in (two, tall)],
            *[pltpu.VMEM((4, *s), BF) for s in (two, tall)],
            *[pltpu.VMEM((4, 2, *s), BF) for s in (two, tall)],
            *[pltpu.VMEM((2, 3, *s), BF) for s in (two, tall)],
            *[pltpu.VMEM((2, *s), BF) for s in (two, tall)],
            pltpu.SemaphoreType.DMA((N_SEND,)),
            pltpu.SemaphoreType.DMA((N_RECV,)),
            pltpu.SemaphoreType.DMA((5,)),
        ],
        compiler_params=pltpu.CompilerParams(
            collective_id=0,
            has_side_effects=True,
            vmem_limit_bytes=63 * 1024 * 1024,
        ),
    )(tokens, out_grad, expert_ids.T, route_weights.T, gate_weight, up_weight, down_weight)
    layer_out, token_grad, route_grad, gate_share, up_share, down_share = pl.pallas_call(
        hand_out,
        out_shape=out_shape,
        in_specs=[vmem] * 6,
        out_specs=(vmem,) * 6,
    )(*results)
    return (layer_out, token_grad, route_grad.T, gate_share, up_share, down_share)


def solution(mesh):
    return jax.shard_map(
        per_device,
        mesh=mesh,
        in_specs=(
            P(("rep", "ep"), None),
            P(("rep", "ep"), None),
            P(("rep", "ep"), None),
            P(("rep", "ep"), None),
            P("ep", None, None),
            P("ep", None, None),
            P("ep", None, None),
        ),
        out_specs=(
            P(("rep", "ep"), None),
            P(("rep", "ep"), None),
            P(("rep", "ep"), None),
            P("ep", "rep", None),
            P("ep", "rep", None),
            P("ep", "rep", None),
        ),
        check_vma=False,
    )
```
